512 devices in a mesh: seq: 8 (over y, core), exp: 16 (over z), hid: 4 (over x).
Axes of the slice: x: 4, y: 4, z: 16, core: 2. Of those that a mesh axis runs over, the one named last changes fastest.
Arguments:
- x_in: bfloat16 [1536, 4096], P(('seq', 'exp', 'hid')), may hold values from -6 to 6
- norm_gain: float32 [4096], replicated, may hold values from 0.1 to 1.9
- w_in_x: bfloat16 [4096, 8192], P('seq', ('exp', 'hid')), may hold values from -0.09375 to 0.09375
- w_in_z: bfloat16 [4096, 8192], P('seq', ('exp', 'hid')), may hold values from -0.09375 to 0.09375
- conv_weight: float32 [4, 8192], P(None, ('exp', 'hid')), may hold values from -3 to 3
- conv_bias: float32 [8192], P(('exp', 'hid')), may hold values from -3 to 3
- w_xproj: bfloat16 [8192, 288], P(('exp', 'hid')), may hold values from -0.125 to 0.125
- w_dt: bfloat16 [256, 8192], P(None, ('exp', 'hid')), may hold values from -0.375 to 0.375
- dt_bias: float32 [8192], P(('exp', 'hid')), may hold values from -5 to -2.5
- a_log: float32 [16, 8192], P(None, ('exp', 'hid')), may hold values from -6 to 3
- d_skip: float32 [8192], P(('exp', 'hid')), may hold values from 0.5 to 1.5
- w_out: bfloat16 [8192, 4096], P(('exp', 'hid'), 'seq'), may hold values from -0.0625 to 0.0625
- moe_gain: float32 [4096], replicated, may hold values from 0.1 to 1.9
- route_ids: int32 [1536, 2], P(('seq', 'exp', 'hid')), may hold values from 0 to 15, all different within a row; in each aligned block of 12 rows (0 to 11, 12 to 23, ...) at most 3 rows name the same one
- route_weights: bfloat16 [1536, 2], P(('seq', 'exp', 'hid')), may hold values from 0.099609375 to 1
- w_gate: bfloat16 [16, 4096, 12288], P('exp', None, ('seq', 'hid')), may hold values from -0.09375 to 0.09375
Outputs:
- resid: bfloat16 [1536, 4096], P(('seq', 'exp', 'hid'))
- expert_act: bfloat16 [16, 384, 12288], P('exp', None, ('seq', 'hid'))
The draws below stay inside these ranges and needn't reach their ends.
Inputs may be any that keep to these rules, and one draw needn't show every extreme that they name: `route_ids`: in each aligned block of 12 tokens no expert is named by more than 3 rows, and in some block one expert is named by exactly 3; a token names 2 different experts.
All inputs are finite; a program needn't handle non-finite values.
Results may differ from the reference program's by a relative error of at most 0.015.
Values may be sent and summed in bfloat16 or wider, within the bound.
No kernel may reach another device: no remote copies, remote signals or barrier semaphores. Data moves between devices by JAX's collectives and lax.ppermute only.
A program may use at most 64 MiB of HBM per device.

```python
import math
import jax
import jax.numpy as jnp
import numpy as np
from jax import lax

D = 4096
INNER = 8192
STATES = 16
CONV = 4
RANK = 256
FF = 12288
TOP = 2
EXPERTS = 16
TOKENS = 1536
BLOCK = 12
MOST = 3
CAP = 384


def block_levels(key, extent, pieces, least, top_value):
    level = 1.0
    for dim, shards_of in pieces:
        heights = jax.random.uniform(jax.random.fold_in(jax.random.fold_in(key, 6), dim), (shards_of,), jnp.float32, least / len(pieces), top_value / len(pieces))
        level = level * jnp.repeat(jnp.exp(heights), extent[dim] // shards_of).reshape((-1,) + (1,) * (len(extent) - 1 - dim))
    return level


def deal_out(key, own, number, rows, number_of, top, bound, lean):
    order = jax.random.permutation(key, number_of)
    crowded, usual = portions_of(number_of, rows * top, bound, lean, True), portions_of(number_of, rows * top, bound, lean, False)
    places = jnp.arange(number_of)

    def named(lengths, rotation):
        used = int((lengths > 0).sum())
        fixed = max(1, used // 4)
        passed = fixed + (places - fixed + rotation * (used - fixed)) % max(1, number_of - fixed)
        return jnp.zeros((number_of,), jnp.int32).at[order[jnp.where(places < fixed, places, passed)]].set(jnp.asarray(lengths, jnp.int32))

    lengths = jnp.where(number % 4 == 0, named(crowded, number // 4), named(usual, number - number // 4 - 1))
    mixed = jax.random.permutation(jax.random.fold_in(own, 3), number_of)
    giver, receiver = mixed[0:number_of // 2 * 2:2], mixed[1:number_of // 2 * 2:2]
    margin = jnp.minimum(lengths[giver] - 1, bound - lengths[receiver]) // 2
    margin = jnp.where((giver == order[0]) | (receiver == order[0]) | (lengths[receiver] == 0), 0, jnp.maximum(margin, 0))
    passed = jax.random.randint(jax.random.fold_in(own, 4), (number_of // 2,), 0, 1 << 20) % (margin + 1)
    lengths = lengths.at[giver].add(-passed).at[receiver].add(passed)
    members = jnp.searchsorted(jnp.cumsum(lengths), jnp.arange(rows * top), side="right").astype(jnp.int32)
    grid = members.reshape(top, rows).T
    grid = grid[jax.random.permutation(jax.random.fold_in(own, 1), rows)]
    rotation = jax.random.randint(jax.random.fold_in(own, 2), (rows, 1), 0, top)
    return jnp.take_along_axis(grid, (jnp.arange(top)[None, :] + rotation) % top, axis=1)


def portions_of(number_of, total, reach, slope, full):
    loads = [(1 << 20) // math.isqrt(standing ** slope) + 1 for standing in range(1, number_of + 1)]
    largest = reach if full else min(reach, max(-(-total // number_of), total * loads[0] // sum(loads)))
    least = 1 if total - largest >= number_of - 1 else 0
    holding, surplus = [largest] + [least] * (number_of - 1), total - largest - least * (number_of - 1)
    while surplus > 0:
        free = [i for i in range(1, number_of) if holding[i] < largest] or [i for i in range(1, number_of) if holding[i] < reach]
        mass, remaining = sum([loads[i] for i in free]), surplus
        for i in free:
            addition = min(reach - holding[i], max(1, remaining * loads[i] // mass), surplus)
            holding[i] = holding[i] + addition
            surplus = surplus - addition
    return np.array(holding)


def scatter_about(stream_key, extent, spread, bound, pieces=(), kind=jnp.bfloat16):
    drawn = spread * jax.random.normal(stream_key, extent, jnp.float32)
    if pieces:
        drawn = drawn * block_levels(stream_key, extent, pieces, -0.22, 0.18)
    return jnp.clip(drawn, -bound, bound).astype(kind)


def setup_inputs(seed: int = 0) -> dict:
    seeds = jax.random.split(jax.random.key(seed), 17)
    x_in = scatter_about(seeds[0], (TOKENS, D), 1.0, 6.0, ((0, 512),))
    norm_gain = jnp.clip(1.0 + 0.18 * jax.random.normal(seeds[1], (D,), jnp.float32), 0.1, 1.9)
    w_in_x = scatter_about(seeds[2], (D, INNER), D ** -0.5, 0.09375, ((0, 8), (1, 64)))
    w_in_z = scatter_about(seeds[3], (D, INNER), D ** -0.5, 0.09375, ((0, 8), (1, 64)))
    conv_weight = scatter_about(seeds[4], (CONV, INNER), 0.5, 3.0, ((1, 64),), jnp.float32)
    conv_bias = scatter_about(seeds[5], (INNER,), 0.5, 3.0, ((0, 64),), jnp.float32)
    w_xproj = scatter_about(seeds[6], (INNER, RANK + 2 * STATES), (INNER // 4) ** -0.5, 0.125, ((0, 64),))
    w_dt = scatter_about(seeds[7], (RANK, INNER), RANK ** -0.5, 0.375, ((1, 64),))
    dt_bias = jnp.clip(-5.0 + 2.5 * jax.random.uniform(seeds[8], (INNER,), jnp.float32) ** block_levels(seeds[8], (INNER,), ((0, 64),), -0.2, 0.2), -5.0, -2.5)
    a_log = jnp.clip(-6.0 + 9.0 * jax.random.uniform(seeds[9], (STATES, INNER), jnp.float32) ** block_levels(seeds[9], (STATES, INNER), ((1, 64),), -0.2, 0.2), -6.0, 3.0)
    d_skip = jnp.clip(0.5 + 1.0 * jax.random.uniform(seeds[10], (INNER,), jnp.float32) ** block_levels(seeds[10], (INNER,), ((0, 64),), -0.2, 0.2), 0.5, 1.5)
    w_out = scatter_about(seeds[11], (INNER, D), INNER ** -0.5, 0.0625, ((0, 64), (1, 8)))
    moe_gain = jnp.clip(1.0 + 0.18 * jax.random.normal(seeds[12], (D,), jnp.float32), 0.1, 1.9)
    route_ids_keys = jax.random.split(jax.random.fold_in(seeds[13], 1), TOKENS // BLOCK)
    route_ids_turns = jax.random.permutation(jax.random.fold_in(seeds[13], 3), TOKENS // BLOCK)
    route_ids = jax.vmap(lambda own, number: deal_out(jax.random.fold_in(seeds[13], 2), own, number, BLOCK, EXPERTS, TOP, MOST, 2))(route_ids_keys, route_ids_turns).reshape((TOKENS, TOP))
    route_weights = jnp.clip(0.099609375 + 0.9003906 * jax.random.uniform(seeds[14], (TOKENS, TOP), jnp.float32) ** block_levels(seeds[14], (TOKENS, TOP), ((0, 512),), -0.2, 0.2), 0.099609375, 1.0).astype(jnp.bfloat16)
    w_gate = scatter_about(seeds[15], (EXPERTS, D, FF), D ** -0.5, 0.09375, ((0, 16), (2, 32)))
    return {"x_in": x_in, "norm_gain": norm_gain, "w_in_x": w_in_x, "w_in_z": w_in_z, "conv_weight": conv_weight, "conv_bias": conv_bias, "w_xproj": w_xproj, "w_dt": w_dt, "dt_bias": dt_bias, "a_log": a_log, "d_skip": d_skip, "w_out": w_out, "moe_gain": moe_gain, "route_ids": route_ids, "route_weights": route_weights, "w_gate": w_gate}


def normalize(values, gain):
    wide = values.astype(jnp.float32)
    scale = lax.rsqrt(lax.optimization_barrier(jnp.mean(wide * wide, axis=-1, keepdims=True)) + 1e-05)
    return (wide * scale * gain).astype(jnp.bfloat16)

def reference(x_in, norm_gain, w_in_x, w_in_z, conv_weight, conv_bias, w_xproj, w_dt, dt_bias, a_log, d_skip, w_out, moe_gain, route_ids, route_weights, w_gate):
    normed = normalize(x_in, norm_gain)
    stream = jnp.dot(normed, w_in_x, preferred_element_type=jnp.float32).astype(jnp.bfloat16)
    gate_in = jnp.dot(normed, w_in_z, preferred_element_type=jnp.float32).astype(jnp.bfloat16)
    padded = jnp.concatenate([jnp.zeros((CONV - 1, INNER), jnp.bfloat16), stream], 0).astype(jnp.float32)
    convolved = conv_bias + jnp.zeros((TOKENS, INNER), jnp.float32)
    for offset in range(CONV):
        convolved = convolved + conv_weight[offset] * padded[offset:offset + TOKENS]
    inner_act = jax.nn.silu(convolved).astype(jnp.bfloat16)
    projected = jnp.dot(inner_act, w_xproj, preferred_element_type=jnp.float32)
    step_low = projected[:, :RANK].astype(jnp.bfloat16)
    input_mat = projected[:, RANK:RANK + STATES]
    output_mat = projected[:, RANK + STATES:]
    step_size = jax.nn.softplus(jnp.dot(step_low, w_dt, preferred_element_type=jnp.float32) + dt_bias)
    decay = -jnp.exp(a_log)
    inner_f = inner_act.astype(jnp.float32)

    def advance(state, inputs):
        step_t, inner_t, in_t, out_t = inputs
        state = jnp.exp(step_t[None, :] * decay) * state + (step_t * inner_t)[None, :] * in_t[:, None]
        return (state, lax.optimization_barrier(jnp.sum(out_t[:, None] * state, 0)))
    start_state = jnp.zeros((STATES, INNER), jnp.float32)
    last_state, ssm = lax.scan(advance, start_state, (step_size, inner_f, input_mat, output_mat))
    ssm = ssm + d_skip * inner_f
    gated = (ssm * jax.nn.silu(gate_in.astype(jnp.float32))).astype(jnp.bfloat16)
    resid = (x_in.astype(jnp.float32) + jnp.dot(gated, w_out, preferred_element_type=jnp.float32)).astype(jnp.bfloat16)
    moe_in = normalize(resid, moe_gain)
    block_total = TOKENS // BLOCK
    route_grid = route_ids.reshape(block_total, BLOCK * TOP).astype(jnp.int32)
    onehot = (route_grid[:, :, None] == jnp.arange(EXPERTS, dtype=jnp.int32)[None, None, :]).astype(jnp.int32)
    running = (jnp.cumsum(onehot, axis=1) - 1).astype(jnp.int32)
    position = lax.optimization_barrier(jnp.sum(running * onehot, axis=2)).astype(jnp.int32)
    slot_index = (jnp.arange(block_total, dtype=jnp.int32)[:, None] * MOST + position).astype(jnp.int32)
    token_index = (jnp.arange(block_total, dtype=jnp.int32)[:, None] * BLOCK + jnp.arange(BLOCK * TOP, dtype=jnp.int32)[None, :] // TOP).astype(jnp.int32)
    source_token = jnp.zeros((EXPERTS, CAP), jnp.int32).at[route_grid, slot_index].set(token_index)
    slot_weight = jnp.zeros((EXPERTS, CAP), jnp.float32).at[route_grid, slot_index].set(route_weights.reshape(block_total, BLOCK * TOP).astype(jnp.float32))

    def one_expert(inputs):
        sources, weights, matrix = inputs
        rows_in = moe_in[sources]
        hidden = jax.nn.silu(jnp.dot(rows_in, matrix, preferred_element_type=jnp.float32))
        return (hidden * weights[:, None]).astype(jnp.bfloat16)
    expert_act = lax.map(one_expert, (source_token, slot_weight, w_gate))
    return (resid, expert_act)
```

```python
import functools

import jax
import jax.numpy as jnp
from jax import lax
from jax.experimental import pallas as pl
from jax.experimental.pallas import tpu as pltpu
from jax.sharding import PartitionSpec as P

F32 = jnp.float32
BF16 = jnp.bfloat16
MOST = 3


def exchange(x, axis):
    return lax.all_to_all(x, axis, split_axis=0, concat_axis=0, tiled=True)


def spread(x, axis):
    n = lax.axis_size(axis)
    return exchange(jnp.broadcast_to(x[None], (n,) + x.shape), axis)


def normalize(values, gain):
    wide = values.astype(F32)
    scale = lax.rsqrt(jnp.mean(wide * wide, axis=-1, keepdims=True) + 1e-05)
    return (wide * scale * gain).astype(BF16)


def softplus(v):
    return jnp.maximum(v, 0.0) + jnp.log1p(jnp.exp(-jnp.abs(v)))


def scan_kernel(low_ref, wdt_ref, bias_ref, alog_ref, act_ref, b_ref, c_ref, out_ref, cum_ref, state_ref, step_s, drive_s):
    tokens = low_ref.shape[0]
    step = softplus(jnp.dot(low_ref[...], wdt_ref[...], preferred_element_type=F32) + bias_ref[...])
    step_s[...] = step
    drive_s[...] = step * act_ref[...].astype(F32)
    decay = -jnp.exp(alog_ref[...])
    states, channels = decay.shape
    state = jnp.zeros((states, channels), F32)
    total = jnp.zeros((1, channels), F32)
    for t in range(tokens):
        step_t = step_s[t : t + 1, :]
        b_t = jnp.broadcast_to(b_ref[:, t : t + 1], (states, channels))
        c_t = jnp.broadcast_to(c_ref[:, t : t + 1], (states, channels))
        state = jnp.exp(step_t * decay) * state + drive_s[t : t + 1, :] * b_t
        total = total + step_t
        out_ref[t : t + 1, :] = jnp.sum(c_t * state, axis=0, keepdims=True)
        cum_ref[t : t + 1, :] = total
    state_ref[...] = state


def gate_kernel(me_ref, all_ref, alog_ref, c_ref, cum_ref, local_ref, act_ref, skip_ref, z_ref, out_ref, corr_s):
    tokens = cum_ref.shape[0]
    decay = -jnp.exp(alog_ref[...])
    states, channels = decay.shape
    state = jnp.zeros((states, channels), F32)
    me = me_ref[0]
    for k in range(all_ref.shape[0] - 1):
        total = all_ref[k, states : states + 1, :]
        later = jnp.exp(total * decay) * state + all_ref[k, 0:states, :]
        state = jnp.where(k < me, later, state)
    for t in range(tokens):
        c_t = jnp.broadcast_to(c_ref[:, t : t + 1], (states, channels))
        term = c_t * (jnp.exp(cum_ref[t : t + 1, :] * decay) * state)
        corr_s[t : t + 1, :] = jnp.sum(term, axis=0, keepdims=True)
    z = z_ref[...].astype(F32)
    ssm = local_ref[...] + corr_s[...] + skip_ref[...] * act_ref[...].astype(F32)
    out_ref[...] = (ssm * (z / (1.0 + jnp.exp(-z)))).astype(BF16)


def shards(
    x_in,
    norm_gain,
    w_in_x,
    w_in_z,
    conv_weight,
    conv_bias,
    w_xproj,
    w_dt,
    dt_bias,
    a_log,
    d_skip,
    w_out,
    moe_gain,
    route_ids,
    route_weights,
    w_gate,
):
    n_seq, n_exp, n_hid = (lax.axis_size(a) for a in ("seq", "exp", "hid"))
    at_seq, at_exp, at_hid = (lax.axis_index(a) for a in ("seq", "exp", "hid"))
    rows, width = x_in.shape
    tokens = rows * n_exp * n_hid
    channels = w_in_x.shape[1]
    states = a_log.shape[0]
    rank = w_dt.shape[0]
    block = rows * n_hid
    half = width // n_hid // 2

    w_in = lax.all_gather(jnp.concatenate([w_in_x, w_in_z], 1), "seq", axis=0, tiled=True)
    route = []
    for s in range(n_seq):
        for h in range(n_hid):
            per = n_seq // n_hid
            route.append((s * n_hid + h, (h * per + s % per) * n_hid + s // per))
    w_out_here = lax.ppermute(w_out, ("seq", "hid"), route)
    swap = [(i, i ^ 1) for i in range(n_seq)]
    w_mine = w_gate[0].reshape(n_hid, 2, half, -1)
    core = at_seq % 2
    w_keep = lax.dynamic_index_in_dim(w_mine, core, 1, keepdims=False)
    w_other = lax.ppermute(lax.dynamic_index_in_dim(w_mine, 1 - core, 1, keepdims=False), "seq", swap)

    routes = jnp.concatenate([route_ids.astype(BF16), route_weights], 1)
    packed = jnp.concatenate([x_in, jnp.pad(routes, ((0, 0), (0, 124)))], 1)
    over_exp = lax.all_gather(packed, "exp", axis=0, tiled=False)
    everything = spread(over_exp, "hid")
    x_all = everything[..., :width]
    routes_all = everything[..., width : width + 4].transpose(1, 0, 2, 3).reshape(n_exp, block, 4).astype(F32)
    normed = normalize(x_all.reshape(tokens, width), norm_gain)
    both = jnp.dot(normed, w_in, preferred_element_type=F32).astype(BF16)
    both = both.reshape(n_hid, n_exp, rows, 2 * channels).transpose(1, 0, 2, 3).reshape(tokens, 2 * channels)
    stream, gate_in = both[:, :channels], both[:, channels:]

    taps = conv_weight.shape[0]
    before = lax.ppermute(stream[tokens - (taps - 1) :], "seq", [(i, i + 1) for i in range(n_seq - 1)])
    padded = jnp.concatenate([before, stream], 0).astype(F32)
    convolved = conv_bias[None] + conv_weight[0] * padded[0:tokens]
    for offset in range(1, taps):
        convolved = convolved + conv_weight[offset] * padded[offset : offset + tokens]
    inner_act = jax.nn.silu(convolved).astype(BF16)

    low_part = jnp.dot(inner_act, w_xproj[:, :rank], preferred_element_type=F32)
    map_part = lax.dot_general(
        w_xproj[:, rank:], inner_act, (((0,), (1,)), ((), ())), preferred_element_type=F32
    )
    low_tiles = low_part.reshape(tokens // 8, 8, rank // 128, 128).transpose(0, 2, 1, 3).reshape(-1, 8, 128)
    map_wide = jnp.pad(map_part, ((0, 0), (0, -tokens % 128)))
    wide = map_wide.shape[1]
    map_tiles = map_wide.reshape(2 * states // 8, 8, wide // 128, 128).transpose(0, 2, 1, 3).reshape(-1, 8, 128)
    n_low, n_map = low_tiles.shape[0], map_tiles.shape[0]
    tiles = jnp.concatenate(
        [low_tiles, map_tiles, jnp.zeros((n_exp * n_hid - n_low - n_map, 8, 128), F32)], 0
    ).astype(BF16)
    got = exchange(tiles, ("exp", "hid"))
    summed = jnp.sum(got.astype(F32), 0).astype(BF16)
    back = spread(summed, ("exp", "hid"))
    step_low = back[:n_low].reshape(tokens // 8, rank // 128, 8, 128).transpose(0, 2, 1, 3).reshape(tokens, rank)
    maps = (
        back[n_low : n_low + n_map]
        .reshape(2 * states // 8, wide // 128, 8, 128)
        .transpose(0, 2, 1, 3)
        .reshape(2 * states, wide)
        .astype(F32)
    )
    input_mat, output_mat = maps[:states], maps[states:]

    local_out, cum, state = pl.pallas_call(
        scan_kernel,
        out_shape=(
            jax.ShapeDtypeStruct((tokens, channels), F32),
            jax.ShapeDtypeStruct((tokens, channels), F32),
            jax.ShapeDtypeStruct((states, channels), F32),
        ),
        scratch_shapes=[pltpu.VMEM((tokens, channels), F32), pltpu.VMEM((tokens, channels), F32)],
        compiler_params=pltpu.CompilerParams(vmem_limit_bytes=32 * 2**20),
        name="scan",
    )(step_low, w_dt, dt_bias[None], a_log, inner_act, input_mat, output_mat)

    rows_ids = routes_all[:, :, :2].reshape(n_exp, -1)
    rows_wts = routes_all[:, :, 2:].reshape(n_exp, -1)
    n_rows = rows_ids.shape[1]
    upto = (jnp.arange(n_rows)[:, None] <= jnp.arange(n_rows)[None, :]).astype(F32)
    named = (rows_ids == at_exp.astype(F32)).astype(F32)
    place = jnp.dot(named, upto) * named
    slot_wts = jnp.stack(
        [jnp.sum(jnp.where(place == i + 1.0, rows_wts, 0.0), 1) for i in range(MOST)], 1
    ).reshape(1, -1)

    carried = jnp.concatenate(
        [
            state,
            cum[tokens - 1 :],
            jnp.pad(slot_wts, ((0, 0), (0, channels - slot_wts.shape[1]))),
            jnp.zeros((6, channels), F32),
        ],
        0,
    )
    carried_all = lax.all_gather(carried, "seq", axis=0, tiled=False)
    weights = carried_all[:, states + 1, : slot_wts.shape[1]].reshape(-1)

    vmem = pl.BlockSpec(memory_space=pltpu.VMEM)
    gated = pl.pallas_call(
        gate_kernel,
        out_shape=jax.ShapeDtypeStruct((tokens, channels), BF16),
        in_specs=[pl.BlockSpec(memory_space=pltpu.SMEM)] + [vmem] * 8,
        out_specs=vmem,
        scratch_shapes=[pltpu.VMEM((tokens, channels), F32)],
        compiler_params=pltpu.CompilerParams(vmem_limit_bytes=32 * 2**20),
        name="gate",
    )(at_seq.astype(jnp.int32)[None], carried_all, a_log, output_mat, cum, local_out, inner_act, d_skip[None], gate_in)

    per = n_seq // n_hid
    w_out_all = lax.all_gather(w_out_here, "seq", axis=0, tiled=False)
    w_out_all = w_out_all.reshape(n_hid, per, channels, -1).transpose(0, 2, 1, 3).reshape(n_hid * channels, -1)
    gated_all = lax.all_gather(gated, "hid", axis=1, tiled=True)
    mixed = jnp.dot(gated_all, w_out_all, preferred_element_type=F32).astype(BF16)
    cols = mixed.shape[1]
    parts = exchange(mixed.reshape(n_exp, block, cols), "exp")
    x_block = lax.dynamic_slice(
        x_all, (0, at_exp, 0, at_hid * cols), (n_hid, 1, rows, cols)
    ).reshape(block, cols)
    resid_part = (x_block.astype(F32) + jnp.sum(parts.astype(F32), 0)).astype(BF16)
    resid_block = lax.all_gather(resid_part, "hid", axis=1, tiled=True)
    resid = lax.dynamic_slice_in_dim(resid_block, at_hid * rows, rows, 0)
    wide_block = resid_block.astype(F32)
    scale = lax.rsqrt(jnp.mean(wide_block * wide_block, axis=-1, keepdims=True) + 1e-05)
    gain = lax.dynamic_slice_in_dim(moe_gain, at_hid * cols, cols, 0)
    moe_in = (resid_part.astype(F32) * scale * gain).astype(BF16)

    ids = lax.dynamic_index_in_dim(rows_ids, at_exp, 0, keepdims=False)
    onehot = (ids[:, None] == jnp.arange(n_exp, dtype=F32)[None, :]).astype(F32)
    position = jnp.sum(jnp.dot(upto.T, onehot) * onehot, 1) - 1.0
    target = ids * MOST + position
    select = (target[None, :] == jnp.arange(n_exp * MOST, dtype=F32)[:, None]).astype(F32)
    select = jnp.sum(select.reshape(n_exp * MOST, block, -1), 2).astype(BF16)
    send = jnp.dot(select, moe_in, preferred_element_type=F32).astype(BF16)
    slots = exchange(send.reshape(n_exp, MOST, cols), "exp").reshape(n_exp * MOST, 2, half)

    halves = jnp.tile(slots.transpose(1, 0, 2), (n_seq // 2, 1, 1))
    seq_slots = exchange(halves, "seq").reshape(-1, half)
    all_slots = spread(seq_slots, "hid")
    dims = (((2,), (1,)), ((0,), (0,)))
    away = jnp.sum(lax.dot_general(all_slots, w_other, dims, preferred_element_type=F32), 0)
    back_here = lax.ppermute(away, "seq", swap)
    home = jnp.sum(lax.dot_general(all_slots, w_keep, dims, preferred_element_type=F32), 0)
    activated = jax.nn.silu(home + back_here) * weights[:, None]
    return (resid, activated.astype(BF16)[None])


def solution(mesh):
    in_specs = (
        P(("seq", "exp", "hid"), None),
        P(),
        P("seq", ("exp", "hid")),
        P("seq", ("exp", "hid")),
        P(None, ("exp", "hid")),
        P(("exp", "hid")),
        P(("exp", "hid"), None),
        P(None, ("exp", "hid")),
        P(("exp", "hid")),
        P(None, ("exp", "hid")),
        P(("exp", "hid")),
        P(("exp", "hid"), "seq"),
        P(),
        P(("seq", "exp", "hid"), None),
        P(("seq", "exp", "hid"), None),
        P("exp", None, ("seq", "hid")),
    )
    out_specs = (P(("seq", "exp", "hid"), None), P("exp", None, ("seq", "hid")))
    return jax.shard_map(shards, mesh=mesh, in_specs=in_specs, out_specs=out_specs, check_vma=False)
```

```python
import jax
import jax.numpy as jnp
from jax import lax
from jax.experimental import pallas as pl
from jax.experimental.pallas import tpu as pltpu
from jax.sharding import PartitionSpec as P

F32 = jnp.float32
BF16 = jnp.bfloat16
MOST = 3
STATES = 16
CONV = 4
TAPS, BIAS, STEP, SKIP = 16, 20, 21, 22


def exchange(x, axis):
    return lax.all_to_all(x, axis, split_axis=0, concat_axis=0, tiled=True)


def softplus(v):
    return jnp.maximum(v, 0.0) + jnp.log1p(jnp.exp(-jnp.abs(v)))


def silu(v):
    return v / (1.0 + jnp.exp(-v))


def call(body, name, out_shape, scratch, *args, scalars=0, unread=0, more=(), limit=40):
    vmem, smem = pl.BlockSpec(memory_space=pltpu.VMEM), pl.BlockSpec(memory_space=pltpu.SMEM)
    return pl.pallas_call(
        body,
        out_shape=out_shape,
        in_specs=[smem] * scalars
        + [vmem] * (len(args) - scalars - unread)
        + [pl.BlockSpec(memory_space=pl.ANY)] * unread,
        out_specs=jax.tree.map(lambda _: vmem, out_shape),
        scratch_shapes=[pltpu.VMEM(shape, F32) for shape in scratch] + list(more),
        compiler_params=pltpu.CompilerParams(vmem_limit_bytes=limit * 2**20),
        name=name,
    )(*args)


def like(shape, dtype):
    return jax.ShapeDtypeStruct(shape, dtype)


def rows_kernel(x_ref, out_ref, rows_s):
    groups, rows, wide = x_ref.shape
    width = wide - 128
    for g in range(groups):
        rows_s[g * rows : (g + 1) * rows, :] = x_ref[g].astype(F32)
    x = rows_s[:, 0:width]
    scale = lax.rsqrt(jnp.mean(x * x, axis=-1, keepdims=True) + 1e-05)
    first = scale.astype(BF16).astype(F32)
    second = (scale - first).astype(BF16).astype(F32)
    more = rows_s[:, width:]
    lane = lax.broadcasted_iota(jnp.int32, more.shape, 1)
    for at, value in enumerate((first, second, scale - first - second)):
        more = jnp.where(lane == 4 + at, value, more)
    rows_s[:, width:] = more
    packed = rows_s[...].astype(BF16)
    for h in range(out_ref.shape[0]):
        out_ref[h] = packed


def project_kernel(x_ref, gain_ref, w_ref, both_ref, tail_ref, route_ref, wide_s, w_s, sem):
    copy = pltpu.make_async_copy(w_ref, w_s, sem)
    copy.start()
    quarters, part, wide = x_ref.shape
    width, both = w_s.shape
    channels = both // 2
    rows = MOST
    groups = part // rows
    block = quarters * rows
    normed = []
    for h in range(quarters):
        more = x_ref[h, :, width:].astype(F32)
        scale = more[:, 4:5] + more[:, 5:6] + more[:, 6:7]
        normed.append((x_ref[h, :, 0:width].astype(F32) * scale * gain_ref[...]).astype(BF16))
        wide_s[2, h * part : (h + 1) * part, :] = more
    copy.wait()
    product = jnp.dot(jnp.concatenate(normed, 0), w_s[...], preferred_element_type=F32)
    wide_s[0] = product[:, :channels]
    wide_s[1] = product[:, channels:]
    for h in range(quarters):
        for r in range(rows):
            source, target = pl.ds(h * part + r, groups, stride=rows), pl.ds(h * rows + r, groups, stride=block)
            for k in range(3):
                wide_s[3 + k, target, :] = wide_s[k, source, :]
    both_ref[0] = wide_s[3].astype(BF16)
    both_ref[1] = wide_s[4].astype(BF16)
    tail_ref[...] = wide_s[3, quarters * part - 8 :, :].astype(BF16).astype(F32)
    route_ref[...] = wide_s[5]


def conv_kernel(stream_ref, halo_ref, params_ref, wx_ref, act_ref, tile_ref, pad_s):
    _, tokens, channels = stream_ref.shape
    pad_s[0:8, :] = halo_ref[...]
    pad_s[8:, :] = stream_ref[0].astype(F32)
    conv = params_ref[BIAS : BIAS + 1, :] + jnp.zeros((tokens, channels), F32)
    for k in range(CONV):
        at = 8 - (CONV - 1) + k
        conv = conv + params_ref[TAPS + k : TAPS + k + 1, :] * pad_s[at : at + tokens, :]
    act = silu(conv).astype(BF16)
    act_ref[...] = act
    rank = wx_ref.shape[1] - 2 * STATES
    low = jnp.dot(act, wx_ref[:, :rank], preferred_element_type=F32)
    maps = lax.dot_general(wx_ref[:, rank:], act, (((0,), (1,)), ((), ())), preferred_element_type=F32)
    n = 0
    for t in range(0, tokens, 8):
        for c in range(0, rank, 128):
            tile_ref[n] = low[t : t + 8, c : c + 128].astype(BF16)
            n += 1
    for s in range(0, 32, 8):
        tile_ref[n] = maps[s : s + 8, 0:128].astype(BF16)
        tile_ref[n + 1] = jnp.concatenate(
            [maps[s : s + 8, 128:tokens], jnp.zeros((8, 256 - tokens), F32)], 1
        ).astype(BF16)
        n += 2
    while n < tile_ref.shape[0]:
        tile_ref[n] = jnp.zeros((8, 128), BF16)
        n += 1


def tile_sum_kernel(got_ref, out_ref):
    total = jnp.sum(got_ref[...].astype(F32), axis=0).astype(BF16)
    out_ref[...] = jnp.broadcast_to(total[None], out_ref.shape)


def scan_kernel(
    back_ref, wdt_ref, params_ref, act_ref, wts_ref, out_ref, cum_ref, c_ref, send_ref, low_s, step_s, drive_s
):
    tokens, rank = low_s.shape
    n = 0
    for t in range(0, tokens, 8):
        for c in range(0, rank, 128):
            low_s[t : t + 8, c : c + 128] = back_ref[n].astype(F32)
            n += 1
    maps = []
    for s in range(0, 32, 8):
        maps.append(jnp.concatenate([back_ref[n].astype(F32), back_ref[n + 1].astype(F32)], 1))
        n += 2
    decay = -jnp.exp(params_ref[0:STATES, :])
    states, channels = decay.shape
    b = jnp.concatenate(maps[:2], 0)
    c = jnp.concatenate(maps[2:], 0)
    c_ref[...] = c
    step = softplus(jnp.dot(low_s[...].astype(BF16), wdt_ref[...], preferred_element_type=F32) + params_ref[STEP : STEP + 1, :])
    step_s[...] = step
    drive_s[...] = step * act_ref[...].astype(F32)
    state = jnp.zeros((states, channels), F32)
    total = jnp.zeros((1, channels), F32)
    for t in range(tokens):
        step_t = step_s[t : t + 1, :]
        b_t = jnp.broadcast_to(b[:, t : t + 1], (states, channels))
        c_t = jnp.broadcast_to(c[:, t : t + 1], (states, channels))
        state = jnp.exp(step_t * decay) * state + drive_s[t : t + 1, :] * b_t
        total = total + step_t
        out_ref[t : t + 1, :] = jnp.sum(c_t * state, axis=0, keepdims=True)
        cum_ref[t : t + 1, :] = total
    row = lax.broadcasted_iota(jnp.int32, (8, channels), 0)
    tail = jnp.where(row == 0, total, jnp.where(row == 1, wts_ref[...], 0.0))
    for k in range(send_ref.shape[0]):
        send_ref[k, 0:states, :] = state
        send_ref[k, states:, :] = tail


def gate_kernel(me_ref, all_ref, params_ref, c_ref, cum_ref, local_ref, act_ref, z_ref, out_ref, corr_s):
    tokens = cum_ref.shape[0]
    decay = -jnp.exp(params_ref[0:STATES, :])
    states, channels = decay.shape
    state = jnp.zeros((states, channels), F32)
    me = me_ref[0]
    for k in range(all_ref.shape[0] - 1):
        total = all_ref[k, states : states + 1, :]
        later = jnp.exp(total * decay) * state + all_ref[k, 0:states, :]
        state = jnp.where(k < me, later, state)
    for t in range(tokens):
        c_t = jnp.broadcast_to(c_ref[:, t : t + 1], (states, channels))
        term = c_t * (jnp.exp(cum_ref[t : t + 1, :] * decay) * state)
        corr_s[t : t + 1, :] = jnp.sum(term, axis=0, keepdims=True)
    z = z_ref[1].astype(F32)
    ssm = local_ref[...] + corr_s[...] + params_ref[SKIP : SKIP + 1, :] * act_ref[...].astype(F32)
    gated = (ssm * silu(z)).astype(BF16)
    for h in range(out_ref.shape[0]):
        out_ref[h] = gated


def mix_kernel(gated_ref, w_ref, out_ref, mixed_s):
    quarters = gated_ref.shape[0]
    per = w_ref.shape[0] // quarters
    cols = w_ref.shape[2]
    for b in range(per):
        total = jnp.dot(gated_ref[0], w_ref[b], preferred_element_type=F32)
        for h in range(1, quarters):
            total = total + jnp.dot(gated_ref[h], w_ref[h * per + b], preferred_element_type=F32)
        mixed_s[:, b * cols : (b + 1) * cols] = total
    block = out_ref.shape[1]
    for j in range(out_ref.shape[0]):
        out_ref[j] = mixed_s[j * block : (j + 1) * block, :].astype(BF16)


def resid_kernel(parts_ref, x_ref, select_ref, resid_ref, send_ref, wide_s):
    block = resid_ref.shape[0]
    total = x_ref[...].astype(F32) + jnp.sum(parts_ref[...].astype(F32), axis=0)
    resid = total.astype(BF16)
    resid_ref[...] = resid
    wide_s[...] = jnp.zeros_like(wide_s)
    wide_s[0:block, :] = resid.astype(F32)
    send = jnp.dot(select_ref[...], wide_s[...].astype(BF16), preferred_element_type=F32)
    most = send_ref.shape[1]
    for e in range(send_ref.shape[0]):
        send_ref[e] = send[e * most : (e + 1) * most].astype(BF16)


def expert_kernel(me_ref, tok_ref, gain_ref, resid_ref, w0_ref, w1_ref, w2_ref, w3_ref, out_ref, w_s, sems):
    me = me_ref[0]
    slots, cols = tok_ref.shape
    quarters = out_ref.shape[0]
    hidden = w_s.shape[1] // quarters
    copies = []
    for d, w_ref in enumerate((w0_ref.at[0, pl.ds(pl.multiple_of(me * cols, cols), cols)], w1_ref, w2_ref, w3_ref)):
        copies.append(pltpu.make_async_copy(w_ref, w_s.at[:, pl.ds(d * hidden, hidden)], sems.at[d]))
        copies[d].start()
    tok = tok_ref[...].astype(F32)
    square = tok * tok
    high = square.astype(BF16)
    low = (square - high.astype(F32)).astype(BF16)
    ones = jnp.ones((16, cols), BF16)
    dims = (((1,), (1,)), ((), ()))
    sums = lax.dot_general(ones, high, dims, preferred_element_type=F32)
    sums = sums + lax.dot_general(ones, low, dims, preferred_element_type=F32)
    first = sums.astype(BF16).astype(F32)
    second = (sums - first).astype(BF16).astype(F32)
    third = sums - first - second
    row = lax.broadcasted_iota(jnp.int32, (16, slots), 0)
    scales = jnp.where(row == 0, first, jnp.where(row == 1, second, third)).astype(BF16)
    resid = resid_ref[...].astype(F32)
    rows = resid.shape[0] // quarters
    for h in range(quarters):
        out_ref[h, slots : slots + 16, :] = scales
        pieces = []
        for r in range(rows):
            own = resid[h * rows + r : h * rows + r + 1, :]
            pieces.append(own[:, 0:hidden])
            pieces.append(own[:, hidden : 2 * hidden])
            pieces.append(jnp.concatenate([own[:, 2 * hidden :], jnp.zeros((1, 3 * hidden - cols), F32)], 1))
        pieces.append(jnp.zeros((16 - len(pieces), hidden), F32))
        out_ref[h, slots + 16 :, :] = jnp.concatenate(pieces, 0).astype(BF16)
    tok = (tok * gain_ref[...]).astype(BF16)
    for d in range(0, quarters, 2):
        copies[d].wait()
        copies[d + 1].wait()
        pair = jnp.dot(tok, w_s[:, d * hidden : (d + 2) * hidden], preferred_element_type=F32).astype(BF16)
        for i in range(2):
            out_ref[lax.rem(me - d - i + quarters, quarters), 0:slots, :] = pair[:, i * hidden : (i + 1) * hidden]


def finish_kernel(part_ref, wts_ref, out_ref, resid_ref, resid_s):
    quarters, _, hidden = part_ref.shape
    slots = out_ref.shape[0]
    rows, width = resid_ref.shape
    cols = width // quarters
    total = jnp.zeros((slots, hidden), F32)
    squares = jnp.zeros((1, slots), F32)
    for q in range(quarters):
        total = total + part_ref[q, 0:slots, :].astype(F32)
        parts = part_ref[q, slots : slots + 16, :].astype(F32)
        squares = squares + (parts[0:1] + parts[1:2] + parts[2:3])
        own = part_ref[q, slots + 16 :, :].astype(F32)
        for r in range(rows):
            for m in range(3):
                size = min(hidden, cols - m * hidden)
                at = q * cols + m * hidden
                resid_s[r : r + 1, at : at + size] = own[3 * r + m : 3 * r + m + 1, 0:size]
    resid_ref[...] = resid_s[0:rows, :].astype(BF16)
    row = lax.broadcasted_iota(jnp.int32, (8, slots), 0)
    scale = lax.rsqrt(squares / width + 1e-05)
    both = jnp.where(row == 0, scale, wts_ref[...]).T
    out_ref[...] = (silu(total * both[:, 0:1]) * both[:, 1:2]).astype(BF16)


def shards(
    x_in,
    norm_gain,
    w_in_x,
    w_in_z,
    conv_weight,
    conv_bias,
    w_xproj,
    w_dt,
    dt_bias,
    a_log,
    d_skip,
    w_out,
    moe_gain,
    route_ids,
    route_weights,
    w_gate,
):
    n_seq, n_exp, n_hid = (lax.axis_size(a) for a in ("seq", "exp", "hid"))
    at_seq, at_exp, at_hid = (lax.axis_index(a) for a in ("seq", "exp", "hid"))
    rows, width = x_in.shape
    tokens = rows * n_exp * n_hid
    channels = w_in_x.shape[1]
    states = a_log.shape[0]
    rank = w_dt.shape[0]
    block = rows * n_hid
    cols = width // n_hid
    per = n_seq // n_hid

    w_in = lax.all_gather(jnp.concatenate([w_in_x, w_in_z], 1), "seq", axis=0, tiled=True)

    own_routes = jnp.concatenate([route_ids.astype(BF16), route_weights], 1)
    own = jnp.concatenate([x_in, jnp.pad(own_routes, ((0, 0), (0, 124)))], 1)
    over_exp = lax.all_gather(own, "exp", axis=0, tiled=False)
    quarter_rows = call(
        rows_kernel,
        "rows",
        like((n_hid, n_exp * rows, width + 128), BF16),
        [(n_exp * rows, width + 128)],
        over_exp,
    )
    quarter_rows, w_out = lax.optimization_barrier((quarter_rows, w_out))
    route = [
        (s * n_hid + h, (h * per + s % per) * n_hid + s // per) for s in range(n_seq) for h in range(n_hid)
    ]
    w_out_here = lax.ppermute(w_out, ("seq", "hid"), route)
    w_out_all = lax.all_gather(w_out_here, "seq", axis=0, tiled=False)
    params = jnp.concatenate(
        [a_log, conv_weight, conv_bias[None], dt_bias[None], d_skip[None], jnp.zeros((1, channels), F32)], 0
    )
    all_rows = exchange(quarter_rows, "hid")
    x_block = lax.dynamic_slice(
        all_rows.reshape(n_hid, n_exp, rows, -1), (0, at_exp, 0, at_hid * cols), (n_hid, 1, rows, cols)
    ).reshape(block, cols)
    both, tail, routes = call(
        project_kernel,
        "project",
        (like((2, tokens, channels), BF16), like((8, channels), F32), like((tokens, 128), F32)),
        [(6, tokens, 128)],
        all_rows,
        norm_gain[None],
        w_in,
        unread=1,
        more=[pltpu.VMEM(w_in.shape, BF16), pltpu.SemaphoreType.DMA],
        limit=58,
    )
    halo = lax.ppermute(tail, "seq", [(i, i + 1) for i in range(n_seq - 1)])
    inner_act, tiles = call(
        conv_kernel,
        "conv",
        (like((tokens, channels), BF16), like((n_exp * n_hid, 8, 128), BF16)),
        [(tokens + 8, channels)],
        both,
        halo,
        params,
        w_xproj,
    )

    got = exchange(tiles, ("exp", "hid"))
    back = exchange(call(tile_sum_kernel, "tile_sum", like(got.shape, BF16), [], got), ("exp", "hid"))

    rows_ids = routes[:, :2].reshape(n_exp, -1)
    rows_wts = routes[:, 2:4].reshape(n_exp, -1)
    n_rows = rows_ids.shape[1]
    upto = (jnp.arange(n_rows)[:, None] <= jnp.arange(n_rows)[None, :]).astype(F32)
    named = (rows_ids == at_exp.astype(F32)).astype(F32)
    place = jnp.dot(named, upto) * named
    slot_wts = jnp.stack(
        [jnp.sum(jnp.where(place == i + 1.0, rows_wts, 0.0), 1) for i in range(MOST)], 1
    ).reshape(1, -1)
    n_slots = slot_wts.shape[1]
    ids = lax.dynamic_index_in_dim(rows_ids, at_exp, 0, keepdims=False)
    onehot = (ids[:, None] == jnp.arange(n_exp, dtype=F32)[None, :]).astype(F32)
    position = jnp.sum(jnp.dot(upto.T, onehot) * onehot, 1) - 1.0
    target = ids * MOST + position
    select = (target[None, :] == jnp.arange(n_exp * MOST, dtype=F32)[:, None]).astype(F32)
    select = jnp.sum(select.reshape(n_exp * MOST, block, -1), 2)
    select = jnp.pad(select, ((0, 0), (0, 16 - block))).astype(BF16)

    local_out, cum, output_mat, carried = call(
        scan_kernel,
        "scan",
        (
            like((tokens, channels), F32),
            like((tokens, channels), F32),
            like((states, 256), F32),
            like((n_seq, states + 8, channels), F32),
        ),
        [(tokens, rank), (tokens, channels), (tokens, channels)],
        back,
        w_dt,
        params,
        inner_act,
        jnp.pad(slot_wts, ((0, 0), (0, channels - n_slots))),
    )
    carried_all = exchange(carried, "seq")
    weights = carried_all[:, states + 1, :n_slots].reshape(1, -1)
    gated = call(
        gate_kernel,
        "gate",
        like((n_hid, tokens, channels), BF16),
        [(tokens, channels)],
        at_seq.astype(jnp.int32)[None],
        carried_all,
        params,
        output_mat,
        cum,
        local_out,
        inner_act,
        both,
        scalars=1,
    )

    gated_all = exchange(gated, "hid")
    mixed = call(mix_kernel, "mix", like((n_exp, block, cols), BF16), [(tokens, cols)], gated_all, w_out_all)
    mixed, w_gate = lax.optimization_barrier((mixed, w_gate))
    w_quarters = w_gate[0].reshape(n_hid, cols, -1)

    def shift(d):
        out = lax.dynamic_index_in_dim(w_quarters, (at_hid + d) % n_hid, 0, keepdims=False)
        return lax.ppermute(out, "hid", [(i, (i + d) % n_hid) for i in range(n_hid)])

    w_1, w_2, w_3 = shift(1), shift(2), shift(3)
    sums = exchange(mixed, "exp")
    resid_part, send = call(
        resid_kernel,
        "resid",
        (like((block, cols), BF16), like((n_exp, MOST, cols), BF16)),
        [(16, cols)],
        sums,
        x_block,
        select,
    )

    slots = exchange(send, "exp").reshape(n_exp * MOST, cols)
    all_slots = lax.all_gather(slots, "seq", axis=0, tiled=True)
    n_all, hidden = all_slots.shape[0], w_gate.shape[2]
    away = call(
        expert_kernel,
        "expert",
        like((n_hid, n_all + 32, hidden), BF16),
        [],
        at_hid.astype(jnp.int32)[None],
        all_slots,
        lax.dynamic_slice_in_dim(moe_gain, at_hid * cols, cols, 0)[None],
        resid_part,
        w_gate,
        w_1,
        w_2,
        w_3,
        scalars=1,
        unread=4,
        more=[pltpu.VMEM((cols, n_hid * hidden), BF16), pltpu.SemaphoreType.DMA((n_hid,))],
        limit=58,
    )
    home = exchange(away, "hid")
    activated, resid = call(
        finish_kernel,
        "finish",
        (like((n_all, hidden), BF16), like((rows, width), BF16)),
        [(8, width)],
        home,
        weights,
    )
    return (resid, activated[None])


def solution(mesh):
    in_specs = (
        P(("seq", "exp", "hid"), None),
        P(),
        P("seq", ("exp", "hid")),
        P("seq", ("exp", "hid")),
        P(None, ("exp", "hid")),
        P(("exp", "hid")),
        P(("exp", "hid"), None),
        P(None, ("exp", "hid")),
        P(("exp", "hid")),
        P(None, ("exp", "hid")),
        P(("exp", "hid")),
        P(("exp", "hid"), "seq"),
        P(),
        P(("seq", "exp", "hid"), None),
        P(("seq", "exp", "hid"), None),
        P("exp", None, ("seq", "hid")),
    )
    out_specs = (P(("seq", "exp", "hid"), None), P("exp", None, ("seq", "hid")))
    return jax.shard_map(shards, mesh=mesh, in_specs=in_specs, out_specs=out_specs, check_vma=False)
```

```python
import jax
import jax.numpy as jnp
from jax import lax
from jax.experimental import pallas as pl
from jax.experimental.pallas import tpu as pltpu
from jax.sharding import PartitionSpec as P

F32 = jnp.float32
BF16 = jnp.bfloat16
MOST = 3
STATES = 16
CONV = 4
TAPS, BIAS, STEP, SKIP = 16, 20, 21, 22


def exchange(x, axis):
    return lax.all_to_all(x, axis, split_axis=0, concat_axis=0, tiled=True)


def softplus(v):
    return jnp.maximum(v, 0.0) + jnp.log1p(jnp.exp(-jnp.abs(v)))


def silu(v):
    return v / (1.0 + jnp.exp(-v))


def call(body, name, out_shape, scratch, *args, scalars=0, unread=0, more=(), limit=40):
    vmem, smem = pl.BlockSpec(memory_space=pltpu.VMEM), pl.BlockSpec(memory_space=pltpu.SMEM)
    return pl.pallas_call(
        body,
        out_shape=out_shape,
        in_specs=[smem] * scalars
        + [vmem] * (len(args) - scalars - unread)
        + [pl.BlockSpec(memory_space=pl.ANY)] * unread,
        out_specs=jax.tree.map(lambda _: vmem, out_shape),
        scratch_shapes=[pltpu.VMEM(shape, F32) for shape in scratch] + list(more),
        compiler_params=pltpu.CompilerParams(vmem_limit_bytes=limit * 2**20),
        name=name,
    )(*args)


def like(shape, dtype):
    return jax.ShapeDtypeStruct(shape, dtype)


def rows_kernel(x_ref, out_ref, rows_s):
    groups, rows, wide = x_ref.shape
    width = wide - 128
    for g in range(groups):
        rows_s[g * rows : (g + 1) * rows, :] = x_ref[g].astype(F32)
    x = rows_s[:, 0:width]
    scale = lax.rsqrt(jnp.mean(x * x, axis=-1, keepdims=True) + 1e-05)
    first = scale.astype(BF16).astype(F32)
    second = (scale - first).astype(BF16).astype(F32)
    more = rows_s[:, width:]
    lane = lax.broadcasted_iota(jnp.int32, more.shape, 1)
    for at, value in enumerate((first, second, scale - first - second)):
        more = jnp.where(lane == 4 + at, value, more)
    rows_s[:, width:] = more
    packed = rows_s[...].astype(BF16)
    for h in range(out_ref.shape[0]):
        out_ref[h] = packed


def normed_rows(x_ref, gain_ref, width):
    normed, extras = [], []
    for h in range(x_ref.shape[0]):
        more = x_ref[h, :, width:].astype(F32)
        scale = more[:, 4:5] + more[:, 5:6] + more[:, 6:7]
        normed.append((x_ref[h, :, 0:width].astype(F32) * scale * gain_ref[...]).astype(BF16))
        extras.append(more)
    return jnp.concatenate(normed, 0), extras


def in_order(source, target, quarters):
    part = source.shape[0] // quarters
    groups = part // MOST
    for h in range(quarters):
        for r in range(MOST):
            own = source[pl.ds(h * part + r, groups, stride=MOST), :]
            target[pl.ds(h * MOST + r, groups, stride=quarters * MOST), :] = own


def project_kernel(x_ref, gain_ref, w_ref, stream_ref, tail_ref, route_ref, mixed_s, more_s, stream_s):
    quarters, part, _ = x_ref.shape
    normed, extras = normed_rows(x_ref, gain_ref, w_ref.shape[0])
    for h in range(quarters):
        more_s[h * part : (h + 1) * part, :] = extras[h]
    mixed_s[...] = jnp.dot(normed, w_ref[...], preferred_element_type=F32)
    in_order(mixed_s, stream_s, quarters)
    in_order(more_s, route_ref, quarters)
    stream_ref[...] = stream_s[...].astype(BF16)
    tail_ref[...] = stream_s[quarters * part - 8 :, :].astype(BF16).astype(F32)


def project_gate_kernel(x_ref, gain_ref, w_ref, gate_ref, mixed_s, gate_s):
    normed, _ = normed_rows(x_ref, gain_ref, w_ref.shape[0])
    mixed_s[...] = jnp.dot(normed, w_ref[...], preferred_element_type=F32)
    in_order(mixed_s, gate_s, x_ref.shape[0])
    gate_ref[...] = gate_s[...].astype(BF16)


def conv_kernel(stream_ref, halo_ref, params_ref, wx_ref, act_ref, tile_ref, pad_s):
    tokens, channels = stream_ref.shape
    pad_s[0:8, :] = halo_ref[...]
    pad_s[8:, :] = stream_ref[...].astype(F32)
    conv = params_ref[BIAS : BIAS + 1, :] + jnp.zeros((tokens, channels), F32)
    for k in range(CONV):
        at = 8 - (CONV - 1) + k
        conv = conv + params_ref[TAPS + k : TAPS + k + 1, :] * pad_s[at : at + tokens, :]
    act = silu(conv).astype(BF16)
    act_ref[...] = act
    rank = wx_ref.shape[1] - 2 * STATES
    low = jnp.dot(act, wx_ref[:, :rank], preferred_element_type=F32)
    maps = lax.dot_general(wx_ref[:, rank:], act, (((0,), (1,)), ((), ())), preferred_element_type=F32)
    n = 0
    for t in range(0, tokens, 8):
        for c in range(0, rank, 128):
            tile_ref[n] = low[t : t + 8, c : c + 128].astype(BF16)
            n += 1
    for s in range(0, 32, 8):
        tile_ref[n] = maps[s : s + 8, 0:128].astype(BF16)
        tile_ref[n + 1] = jnp.concatenate(
            [maps[s : s + 8, 128:tokens], jnp.zeros((8, 256 - tokens), F32)], 1
        ).astype(BF16)
        n += 2
    while n < tile_ref.shape[0]:
        tile_ref[n] = jnp.zeros((8, 128), BF16)
        n += 1


def tile_sum_kernel(got_ref, out_ref):
    total = jnp.sum(got_ref[...].astype(F32), axis=0).astype(BF16)
    out_ref[...] = jnp.broadcast_to(total[None], out_ref.shape)


def scan_kernel(
    back_ref, wdt_ref, params_ref, act_ref, wts_ref, out_ref, send_ref, low_s, step_s, drive_s
):
    tokens, rank = low_s.shape
    n = 0
    for t in range(0, tokens, 8):
        for c in range(0, rank, 128):
            low_s[t : t + 8, c : c + 128] = back_ref[n].astype(F32)
            n += 1
    maps = []
    for s in range(0, 32, 8):
        maps.append(jnp.concatenate([back_ref[n].astype(F32), back_ref[n + 1].astype(F32)], 1))
        n += 2
    decay = -jnp.exp(params_ref[0:STATES, :])
    states, channels = decay.shape
    b = jnp.concatenate(maps[:2], 0)
    c = jnp.concatenate(maps[2:], 0)
    out_ref[2 * tokens : 2 * tokens + states, :] = c[:, :channels]
    out_ref[2 * tokens + states :, :] = c[:, channels:]
    step = softplus(jnp.dot(low_s[...].astype(BF16), wdt_ref[...], preferred_element_type=F32) + params_ref[STEP : STEP + 1, :])
    step_s[...] = step
    act = act_ref[...].astype(F32)
    drive_s[...] = step * act
    state = jnp.zeros((states, channels), F32)
    total = jnp.zeros((1, channels), F32)
    for t in range(tokens):
        step_t = step_s[t : t + 1, :]
        b_t = jnp.broadcast_to(b[:, t : t + 1], (states, channels))
        c_t = jnp.broadcast_to(c[:, t : t + 1], (states, channels))
        state = jnp.exp(step_t * decay) * state + drive_s[t : t + 1, :] * b_t
        total = total + step_t
        out_ref[t : t + 1, :] = jnp.sum(c_t * state, axis=0, keepdims=True)
        out_ref[tokens + t : tokens + t + 1, :] = total
    out_ref[0:tokens, :] = out_ref[0:tokens, :] + params_ref[SKIP : SKIP + 1, :] * act
    row = lax.broadcasted_iota(jnp.int32, (8, channels), 0)
    tail = jnp.where(row == 0, total, jnp.where(row == 1, wts_ref[...], 0.0))
    for k in range(send_ref.shape[0]):
        send_ref[k, 0:states, :] = state
        send_ref[k, states:, :] = tail


def gate_kernel(me_ref, all_ref, params_ref, local_ref, z_ref, out_ref, corr_s):
    tokens = z_ref.shape[0]
    decay = -jnp.exp(params_ref[0:STATES, :])
    states, channels = decay.shape
    state = jnp.zeros((states, channels), F32)
    me = me_ref[0]
    for k in range(all_ref.shape[0] - 1):
        total = all_ref[k, states : states + 1, :]
        later = jnp.exp(total * decay) * state + all_ref[k, 0:states, :]
        state = jnp.where(k < me, later, state)
    c = [local_ref[at : at + states, :] for at in (2 * tokens, 2 * tokens + states)]
    for t in range(tokens):
        c_t = jnp.broadcast_to(c[t // channels][:, t % channels : t % channels + 1], (states, channels))
        term = c_t * (jnp.exp(local_ref[tokens + t : tokens + t + 1, :] * decay) * state)
        corr_s[t : t + 1, :] = jnp.sum(term, axis=0, keepdims=True)
    z = z_ref[...].astype(F32)
    ssm = local_ref[0:tokens, :] + corr_s[...]
    gated = (ssm * silu(z)).astype(BF16)
    for h in range(out_ref.shape[0]):
        out_ref[h] = gated


def mix_kernel(gated_ref, w_ref, _0, _1, out_ref, mixed_s):
    quarters = gated_ref.shape[0]
    per = w_ref.shape[0] // quarters
    cols = w_ref.shape[2]
    for b in range(per):
        total = jnp.dot(gated_ref[0], w_ref[b], preferred_element_type=F32)
        for h in range(1, quarters):
            total = total + jnp.dot(gated_ref[h], w_ref[h * per + b], preferred_element_type=F32)
        mixed_s[:, b * cols : (b + 1) * cols] = total
    block = mixed_s.shape[0] // out_ref.shape[0]
    wide = mixed_s.shape[1]
    for j in range(out_ref.shape[0]):
        own = mixed_s[j * block : (j + 1) * block, :]
        rest = jnp.concatenate([own[8:, : wide // 2], own[8:, wide // 2 :]], 0)
        out_ref[j] = jnp.concatenate([own[:8], rest], 1).astype(BF16)


def resid_kernel(parts_ref, x_ref, select_ref, resid_ref, send_ref, wide_s):
    block, cols = resid_ref.shape
    sums = jnp.sum(parts_ref[...].astype(F32), axis=0)
    rest = jnp.concatenate([sums[: block - 8, cols:], sums[block - 8 :, cols:]], 1)
    total = x_ref[...].astype(F32) + jnp.concatenate([sums[:, :cols], rest], 0)
    resid = total.astype(BF16)
    resid_ref[...] = resid
    wide_s[...] = jnp.zeros_like(wide_s)
    wide_s[0:block, :] = resid.astype(F32)
    send = jnp.dot(select_ref[...], wide_s[...].astype(BF16), preferred_element_type=F32)
    for e in range(send_ref.shape[0]):
        own = send[e * MOST : (e + 1) * MOST]
        rows = [own[:, 0:384], own[:, 384:768]]
        rows.append(jnp.concatenate([own[0:1, 768:], own[2:3, 768:896]], 1))
        rows.append(jnp.concatenate([own[1:2, 768:], own[2:3, 896:]], 1))
        send_ref[e] = jnp.concatenate(rows, 0).astype(BF16)


def slots_kernel(got_ref, _0, out_ref, slots_s):
    for j in range(got_ref.shape[0]):
        own = got_ref[j].astype(F32)
        at = j * MOST
        slots_s[at : at + 3, 0:384] = own[0:3]
        slots_s[at : at + 3, 384:768] = own[3:6]
        slots_s[at : at + 1, 768:] = own[6:7, 0:256]
        slots_s[at + 1 : at + 2, 768:] = own[7:8, 0:256]
        slots_s[at + 2 : at + 3, 768:] = jnp.concatenate([own[6:7, 256:], own[7:8, 256:]], 1)
    out_ref[...] = slots_s[...].astype(BF16)


def stage_kernel(me_ref, w0_ref, w1_ref, w2_ref, w3_ref, out_ref, sems):
    cols = out_ref.shape[0]
    hidden = w1_ref.shape[1]
    sources = [w0_ref.at[0, pl.ds(pl.multiple_of(me_ref[0] * cols, cols), cols)], w1_ref, w2_ref, w3_ref]
    copies = []
    for d, w_ref in enumerate(sources):
        copies.append(pltpu.make_async_copy(w_ref, out_ref.at[:, pl.ds(d * hidden, hidden)], sems.at[d]))
        copies[d].start()
    for copy in copies:
        copy.wait()


def expert_kernel(me_ref, tok_ref, gain_ref, resid_ref, w_ref, out_ref):
    me = me_ref[0]
    slots, cols = tok_ref.shape
    quarters = out_ref.shape[0]
    hidden = w_ref.shape[1] // quarters
    tok = tok_ref[...].astype(F32)
    sums = jnp.sum(tok * tok, axis=-1, keepdims=True)
    sums = jnp.broadcast_to(sums, (slots, 128)).T[0:MOST]
    first = sums.astype(BF16).astype(F32)
    second = (sums - first).astype(BF16).astype(F32)
    third = sums - first - second
    row = lax.broadcasted_iota(jnp.int32, (MOST, slots), 0)
    scales = jnp.where(row == 0, first, jnp.where(row == 1, second, third))
    resid = resid_ref[...].astype(F32)
    rows = resid.shape[0] // quarters
    for h in range(quarters):
        pieces = [scales]
        for r in range(rows):
            own = resid[h * rows + r : h * rows + r + 1, :]
            pieces.append(own[:, 0:hidden])
            pieces.append(own[:, hidden : 2 * hidden])
            pieces.append(jnp.concatenate([own[:, 2 * hidden :], jnp.zeros((1, 3 * hidden - cols), F32)], 1))
        pieces.append(jnp.zeros((16 - 4 * MOST, hidden), F32))
        out_ref[h, slots:, :] = jnp.concatenate(pieces, 0).astype(BF16)
    tok = (tok * gain_ref[...]).astype(BF16)
    for d in range(0, quarters, 2):
        pair = jnp.dot(tok, w_ref[:, d * hidden : (d + 2) * hidden], preferred_element_type=F32).astype(BF16)
        for i in range(2):
            out_ref[lax.rem(me - d - i + quarters, quarters), 0:slots, :] = pair[:, i * hidden : (i + 1) * hidden]


def finish_kernel(part_ref, wts_ref, out_ref, resid_ref, resid_s):
    quarters, _, hidden = part_ref.shape
    slots = out_ref.shape[0]
    rows, width = resid_ref.shape
    cols = width // quarters
    total = jnp.zeros((slots, hidden), F32)
    squares = jnp.zeros((1, slots), F32)
    for q in range(quarters):
        total = total + part_ref[q, 0:slots, :].astype(F32)
        own = part_ref[q, slots:, :].astype(F32)
        squares = squares + (own[0:1] + own[1:2] + own[2:3])
        for r in range(rows):
            for m in range(3):
                size = min(hidden, cols - m * hidden)
                at = q * cols + m * hidden
                resid_s[r : r + 1, at : at + size] = own[3 + 3 * r + m : 4 + 3 * r + m, 0:size]
    resid_ref[...] = resid_s[0:rows, :].astype(BF16)
    row = lax.broadcasted_iota(jnp.int32, (8, slots), 0)
    scale = lax.rsqrt(squares / width + 1e-05)
    both = jnp.where(row == 0, scale, wts_ref[...]).T
    out_ref[...] = (silu(total * both[:, 0:1]) * both[:, 1:2]).astype(BF16)


def shards(
    x_in,
    norm_gain,
    w_in_x,
    w_in_z,
    conv_weight,
    conv_bias,
    w_xproj,
    w_dt,
    dt_bias,
    a_log,
    d_skip,
    w_out,
    moe_gain,
    route_ids,
    route_weights,
    w_gate,
):
    n_seq, n_exp, n_hid = (lax.axis_size(a) for a in ("seq", "exp", "hid"))
    at_seq, at_exp, at_hid = (lax.axis_index(a) for a in ("seq", "exp", "hid"))
    rows, width = x_in.shape
    tokens = rows * n_exp * n_hid
    channels = w_in_x.shape[1]
    states = a_log.shape[0]
    rank = w_dt.shape[0]
    block = rows * n_hid
    cols = width // n_hid
    per = n_seq // n_hid

    w_x = lax.all_gather(w_in_x, "seq", axis=0, tiled=True)

    own_routes = jnp.concatenate([route_ids.astype(BF16), route_weights], 1)
    own = jnp.concatenate([x_in, jnp.pad(own_routes, ((0, 0), (0, 124)))], 1)
    over_exp = lax.all_gather(own, "exp", axis=0, tiled=False)
    quarter_rows = call(
        rows_kernel,
        "rows",
        like((n_hid, n_exp * rows, width + 128), BF16),
        [(n_exp * rows, width + 128)],
        over_exp,
    )
    quarter_rows, w_out, w_in_z = lax.optimization_barrier((quarter_rows, w_out, w_in_z))
    w_z = lax.all_gather(w_in_z, "seq", axis=0, tiled=True)
    route = [
        (s * n_hid + h, (h * per + s % per) * n_hid + s // per) for s in range(n_seq) for h in range(n_hid)
    ]
    w_out_here = lax.ppermute(w_out, ("seq", "hid"), route)
    w_out_all = lax.all_gather(w_out_here, "seq", axis=0, tiled=False)
    params = jnp.concatenate(
        [a_log, conv_weight, conv_bias[None], dt_bias[None], d_skip[None], jnp.zeros((1, channels), F32)], 0
    )
    all_rows = exchange(quarter_rows, "hid")
    x_block = lax.dynamic_slice(
        all_rows.reshape(n_hid, n_exp, rows, -1), (0, at_exp, 0, at_hid * cols), (n_hid, 1, rows, cols)
    ).reshape(block, cols)
    stream, tail, routes = call(
        project_kernel,
        "project",
        (like((tokens, channels), BF16), like((8, channels), F32), like((tokens, 128), F32)),
        [(tokens, channels), (tokens, 128), (tokens, channels)],
        all_rows,
        norm_gain[None],
        w_x,
    )
    gate_in = call(
        project_gate_kernel,
        "project_gate",
        like((tokens, channels), BF16),
        [(tokens, channels), (tokens, channels)],
        all_rows,
        norm_gain[None],
        w_z,
    )
    halo = lax.ppermute(tail, "seq", [(i, i + 1) for i in range(n_seq - 1)])
    inner_act, tiles = call(
        conv_kernel,
        "conv",
        (like((tokens, channels), BF16), like((n_exp * n_hid, 8, 128), BF16)),
        [(tokens + 8, channels)],
        stream,
        halo,
        params,
        w_xproj,
    )

    got = exchange(tiles, ("exp", "hid"))
    back = exchange(call(tile_sum_kernel, "tile_sum", like(got.shape, BF16), [], got), ("exp", "hid"))

    rows_ids = routes[:, :2].reshape(n_exp, -1)
    rows_wts = routes[:, 2:4].reshape(n_exp, -1)
    n_rows = rows_ids.shape[1]
    upto = (jnp.arange(n_rows)[:, None] <= jnp.arange(n_rows)[None, :]).astype(F32)
    named = (rows_ids == at_exp.astype(F32)).astype(F32)
    place = jnp.dot(named, upto) * named
    slot_wts = jnp.stack(
        [jnp.sum(jnp.where(place == i + 1.0, rows_wts, 0.0), 1) for i in range(MOST)], 1
    ).reshape(1, -1)
    n_slots = slot_wts.shape[1]
    ids = lax.dynamic_index_in_dim(rows_ids, at_exp, 0, keepdims=False)
    onehot = (ids[:, None] == jnp.arange(n_exp, dtype=F32)[None, :]).astype(F32)
    position = jnp.sum(jnp.dot(upto.T, onehot) * onehot, 1) - 1.0
    target = ids * MOST + position
    select = (target[None, :] == jnp.arange(n_exp * MOST, dtype=F32)[:, None]).astype(F32)
    select = jnp.sum(select.reshape(n_exp * MOST, block, -1), 2)
    select = jnp.pad(select, ((0, 0), (0, 16 - block))).astype(BF16)

    def shift(w, d):
        out = lax.dynamic_index_in_dim(w[0].reshape(n_hid, cols, -1), (at_hid + d) % n_hid, 0, keepdims=False)
        return lax.ppermute(out, "hid", [(i, (i + d) % n_hid) for i in range(n_hid)])

    slot_wts, w_first = lax.optimization_barrier((slot_wts, w_gate))
    w_1, w_3 = shift(w_first, 1), shift(w_first, 3)
    local, carried = call(
        scan_kernel,
        "scan",
        (
            like((2 * tokens + 2 * states, channels), F32),
            like((n_seq, states + 8, channels), F32),
        ),
        [(tokens, rank), (tokens, channels), (tokens, channels)],
        back,
        w_dt,
        params,
        inner_act,
        jnp.pad(slot_wts, ((0, 0), (0, channels - n_slots))),
    )
    carried_all = exchange(carried, "seq")
    weights = carried_all[:, states + 1, :n_slots].reshape(1, -1)
    gated = call(
        gate_kernel,
        "gate",
        like((n_hid, tokens, channels), BF16),
        [(tokens, channels)],
        at_seq.astype(jnp.int32)[None],
        carried_all,
        params,
        local,
        gate_in,
        scalars=1,
    )

    gated_all = exchange(gated, "hid")
    mixed = call(
        mix_kernel,
        "mix",
        like((n_exp, 8, block * cols // 8), BF16),
        [(tokens, cols)],
        gated_all,
        w_out_all,
        w_1,
        w_3,
        unread=2,
    )
    mixed, w_second = lax.optimization_barrier((mixed, w_gate))
    w_2 = shift(w_second, 2)
    sums = exchange(mixed, "exp")
    resid_part, send = call(
        resid_kernel,
        "resid",
        (like((block, cols), BF16), like((n_exp, 8, MOST * cols // 8), BF16)),
        [(16, cols)],
        sums,
        x_block,
        select,
    )

    hidden = w_gate.shape[2]
    w_side = call(
        stage_kernel,
        "stage",
        like((cols, n_hid * hidden), BF16),
        [],
        at_hid.astype(jnp.int32)[None],
        w_gate,
        w_1,
        w_2,
        w_3,
        scalars=1,
        unread=4,
        more=[pltpu.SemaphoreType.DMA((n_hid,))],
    )
    slots = call(
        slots_kernel,
        "slots",
        like((n_exp * MOST, cols), BF16),
        [(n_exp * MOST, cols)],
        exchange(send, "exp"),
        w_side,
        unread=1,
    )
    all_slots = lax.all_gather(slots, "seq", axis=0, tiled=True)
    n_all = all_slots.shape[0]
    away = call(
        expert_kernel,
        "expert",
        like((n_hid, n_all + 16, hidden), BF16),
        [],
        at_hid.astype(jnp.int32)[None],
        all_slots,
        lax.dynamic_slice_in_dim(moe_gain, at_hid * cols, cols, 0)[None],
        resid_part,
        w_side,
        scalars=1,
    )
    home = exchange(away, "hid")
    activated, resid = call(
        finish_kernel,
        "finish",
        (like((n_all, hidden), BF16), like((rows, width), BF16)),
        [(8, width)],
        home,
        weights,
    )
    return (resid, activated[None])


def solution(mesh):
    in_specs = (
        P(("seq", "exp", "hid"), None),
        P(),
        P("seq", ("exp", "hid")),
        P("seq", ("exp", "hid")),
        P(None, ("exp", "hid")),
        P(("exp", "hid")),
        P(("exp", "hid"), None),
        P(None, ("exp", "hid")),
        P(("exp", "hid")),
        P(None, ("exp", "hid")),
        P(("exp", "hid")),
        P(("exp", "hid"), "seq"),
        P(),
        P(("seq", "exp", "hid"), None),
        P(("seq", "exp", "hid"), None),
        P("exp", None, ("seq", "hid")),
    )
    out_specs = (P(("seq", "exp", "hid"), None), P("exp", None, ("seq", "hid")))
    return jax.shard_map(shards, mesh=mesh, in_specs=in_specs, out_specs=out_specs, check_vma=False)
```

```python
import jax
import jax.numpy as jnp
from jax import lax
from jax.experimental import pallas as pl
from jax.experimental.pallas import tpu as pltpu
from jax.sharding import PartitionSpec as P

F32 = jnp.float32
BF16 = jnp.bfloat16
MOST = 3
STATES = 16
CONV = 4
TAPS, BIAS, STEP, SKIP = 16, 20, 21, 22


def exchange(x, axis):
    return lax.all_to_all(x, axis, split_axis=0, concat_axis=0, tiled=True)


def softplus(v):
    return jnp.maximum(v, 0.0) + jnp.log1p(jnp.exp(-jnp.abs(v)))


def silu(v):
    return v / (1.0 + jnp.exp(-v))


def call(body, name, out_shape, scratch, *args, scalars=0, unread=0, more=(), limit=40):
    vmem, smem = pl.BlockSpec(memory_space=pltpu.VMEM), pl.BlockSpec(memory_space=pltpu.SMEM)
    return pl.pallas_call(
        body,
        out_shape=out_shape,
        in_specs=[smem] * scalars
        + [vmem] * (len(args) - scalars - unread)
        + [pl.BlockSpec(memory_space=pl.ANY)] * unread,
        out_specs=jax.tree.map(lambda _: vmem, out_shape),
        scratch_shapes=[pltpu.VMEM(shape, F32) for shape in scratch] + list(more),
        compiler_params=pltpu.CompilerParams(vmem_limit_bytes=limit * 2**20),
        name=name,
    )(*args)


def near_kernel(x_ref, out_ref, sem):
    copy = pltpu.make_async_copy(x_ref, out_ref, sem)
    copy.start()
    copy.wait()


def near(x, name):
    return call(near_kernel, name, like(x.shape, x.dtype), [], x, unread=1, more=[pltpu.SemaphoreType.DMA])


def like(shape, dtype):
    return jax.ShapeDtypeStruct(shape, dtype)


def rows_kernel(x_ref, out_ref, rows_s):
    groups, rows, wide = x_ref.shape
    width = wide - 128
    for g in range(groups):
        rows_s[g * rows : (g + 1) * rows, :] = x_ref[g].astype(F32)
    x = rows_s[:, 0:width]
    scale = lax.rsqrt(jnp.mean(x * x, axis=-1, keepdims=True) + 1e-05)
    first = scale.astype(BF16).astype(F32)
    second = (scale - first).astype(BF16).astype(F32)
    more = rows_s[:, width:]
    lane = lax.broadcasted_iota(jnp.int32, more.shape, 1)
    for at, value in enumerate((first, second, scale - first - second)):
        more = jnp.where(lane == 4 + at, value, more)
    rows_s[:, width:] = more
    packed = rows_s[...].astype(BF16)
    for h in range(out_ref.shape[0]):
        out_ref[h] = packed


def normed_rows(x_ref, gain_ref, width):
    normed, extras = [], []
    for h in range(x_ref.shape[0]):
        more = x_ref[h, :, width:].astype(F32)
        scale = more[:, 4:5] + more[:, 5:6] + more[:, 6:7]
        normed.append((x_ref[h, :, 0:width].astype(F32) * scale * gain_ref[...]).astype(BF16))
        extras.append(more)
    return jnp.concatenate(normed, 0), extras


def in_order(source, target, quarters):
    part = source.shape[0] // quarters
    groups = part // MOST
    for h in range(quarters):
        for r in range(MOST):
            own = source[pl.ds(h * part + r, groups, stride=MOST), :]
            target[pl.ds(h * MOST + r, groups, stride=quarters * MOST), :] = own


def project_kernel(x_ref, gain_ref, w_ref, stream_ref, tail_ref, route_ref, mixed_s, more_s, stream_s):
    quarters, part, _ = x_ref.shape
    normed, extras = normed_rows(x_ref, gain_ref, w_ref.shape[0])
    for h in range(quarters):
        more_s[h * part : (h + 1) * part, :] = extras[h]
    mixed_s[...] = jnp.dot(normed, w_ref[...], preferred_element_type=F32)
    in_order(mixed_s, stream_s, quarters)
    in_order(more_s, route_ref, quarters)
    stream_ref[...] = stream_s[...].astype(BF16)
    tail_ref[...] = stream_s[quarters * part - 8 :, :].astype(BF16).astype(F32)


def project_gate_kernel(x_ref, gain_ref, w_ref, gate_ref, mixed_s, gate_s):
    normed, _ = normed_rows(x_ref, gain_ref, w_ref.shape[0])
    mixed_s[...] = jnp.dot(normed, w_ref[...], preferred_element_type=F32)
    in_order(mixed_s, gate_s, x_ref.shape[0])
    gate_ref[...] = gate_s[...].astype(BF16)


def conv_kernel(stream_ref, halo_ref, params_ref, wx_ref, act_ref, tile_ref, pad_s):
    tokens, channels = stream_ref.shape
    pad_s[0:8, :] = halo_ref[...]
    pad_s[8:, :] = stream_ref[...].astype(F32)
    conv = params_ref[BIAS : BIAS + 1, :] + jnp.zeros((tokens, channels), F32)
    for k in range(CONV):
        at = 8 - (CONV - 1) + k
        conv = conv + params_ref[TAPS + k : TAPS + k + 1, :] * pad_s[at : at + tokens, :]
    act = silu(conv).astype(BF16)
    act_ref[...] = act
    rank = wx_ref.shape[1] - 2 * STATES
    low = jnp.dot(act, wx_ref[:, :rank], preferred_element_type=F32)
    maps = lax.dot_general(wx_ref[:, rank:], act, (((0,), (1,)), ((), ())), preferred_element_type=F32)
    n = 0
    for t in range(0, tokens, 8):
        for c in range(0, rank, 128):
            tile_ref[n] = low[t : t + 8, c : c + 128].astype(BF16)
            n += 1
    for s in range(0, 32, 8):
        tile_ref[n] = maps[s : s + 8, 0:128].astype(BF16)
        tile_ref[n + 1] = jnp.concatenate(
            [maps[s : s + 8, 128:tokens], jnp.zeros((8, 256 - tokens), F32)], 1
        ).astype(BF16)
        n += 2
    while n < tile_ref.shape[0]:
        tile_ref[n] = jnp.zeros((8, 128), BF16)
        n += 1


def tile_sum_kernel(got_ref, out_ref):
    total = jnp.sum(got_ref[...].astype(F32), axis=0).astype(BF16)
    out_ref[...] = jnp.broadcast_to(total[None], out_ref.shape)


def scan_kernel(
    back_ref, wdt_ref, params_ref, act_ref, wts_ref, out_ref, send_ref, low_s, step_s, drive_s
):
    tokens, rank = low_s.shape
    n = 0
    for t in range(0, tokens, 8):
        for c in range(0, rank, 128):
            low_s[t : t + 8, c : c + 128] = back_ref[n].astype(F32)
            n += 1
    maps = []
    for s in range(0, 32, 8):
        maps.append(jnp.concatenate([back_ref[n].astype(F32), back_ref[n + 1].astype(F32)], 1))
        n += 2
    decay = -jnp.exp(params_ref[0:STATES, :])
    states, channels = decay.shape
    b = jnp.concatenate(maps[:2], 0)
    c = jnp.concatenate(maps[2:], 0)
    out_ref[2 * tokens : 2 * tokens + states, :] = c[:, :channels]
    out_ref[2 * tokens + states :, :] = c[:, channels:]
    step = softplus(jnp.dot(low_s[...].astype(BF16), wdt_ref[...], preferred_element_type=F32) + params_ref[STEP : STEP + 1, :])
    step_s[...] = step
    act = act_ref[...].astype(F32)
    drive_s[...] = step * act
    state = jnp.zeros((states, channels), F32)
    total = jnp.zeros((1, channels), F32)
    for t in range(tokens):
        step_t = step_s[t : t + 1, :]
        b_t = jnp.broadcast_to(b[:, t : t + 1], (states, channels))
        c_t = jnp.broadcast_to(c[:, t : t + 1], (states, channels))
        state = jnp.exp(step_t * decay) * state + drive_s[t : t + 1, :] * b_t
        total = total + step_t
        out_ref[t : t + 1, :] = jnp.sum(c_t * state, axis=0, keepdims=True)
        out_ref[tokens + t : tokens + t + 1, :] = total
    out_ref[0:tokens, :] = out_ref[0:tokens, :] + params_ref[SKIP : SKIP + 1, :] * act
    row = lax.broadcasted_iota(jnp.int32, (8, channels), 0)
    tail = jnp.where(row == 0, total, jnp.where(row == 1, wts_ref[...], 0.0))
    for k in range(send_ref.shape[0]):
        send_ref[k, 0:states, :] = state
        send_ref[k, states:, :] = tail


def gate_kernel(me_ref, all_ref, params_ref, local_ref, z_ref, out_ref, corr_s):
    tokens = z_ref.shape[0]
    decay = -jnp.exp(params_ref[0:STATES, :])
    states, channels = decay.shape
    state = jnp.zeros((states, channels), F32)
    me = me_ref[0]
    for k in range(all_ref.shape[0] - 1):
        total = all_ref[k, states : states + 1, :]
        later = jnp.exp(total * decay) * state + all_ref[k, 0:states, :]
        state = jnp.where(k < me, later, state)
    c = [local_ref[at : at + states, :] for at in (2 * tokens, 2 * tokens + states)]
    for t in range(tokens):
        c_t = jnp.broadcast_to(c[t // channels][:, t % channels : t % channels + 1], (states, channels))
        term = c_t * (jnp.exp(local_ref[tokens + t : tokens + t + 1, :] * decay) * state)
        corr_s[t : t + 1, :] = jnp.sum(term, axis=0, keepdims=True)
    z = z_ref[...].astype(F32)
    ssm = local_ref[0:tokens, :] + corr_s[...]
    gated = (ssm * silu(z)).astype(BF16)
    for h in range(out_ref.shape[0]):
        out_ref[h] = gated


def mix_kernel(gated_ref, w_ref, _0, out_ref, mixed_s):
    quarters = gated_ref.shape[0]
    per = w_ref.shape[0] // quarters
    cols = w_ref.shape[2]
    for b in range(per):
        total = jnp.dot(gated_ref[0], w_ref[b], preferred_element_type=F32)
        for h in range(1, quarters):
            total = total + jnp.dot(gated_ref[h], w_ref[h * per + b], preferred_element_type=F32)
        mixed_s[:, b * cols : (b + 1) * cols] = total
    block = mixed_s.shape[0] // out_ref.shape[0]
    wide = mixed_s.shape[1]
    for j in range(out_ref.shape[0]):
        own = mixed_s[j * block : (j + 1) * block, :]
        rest = jnp.concatenate([own[8:, : wide // 2], own[8:, wide // 2 :]], 0)
        out_ref[j] = jnp.concatenate([own[:8], rest], 1).astype(BF16)


def resid_kernel(parts_ref, x_ref, select_ref, resid_ref, send_ref, wide_s):
    block, cols = resid_ref.shape
    sums = jnp.sum(parts_ref[...].astype(F32), axis=0)
    rest = jnp.concatenate([sums[: block - 8, cols:], sums[block - 8 :, cols:]], 1)
    total = x_ref[...].astype(F32) + jnp.concatenate([sums[:, :cols], rest], 0)
    resid = total.astype(BF16)
    resid_ref[...] = resid
    wide_s[...] = jnp.zeros_like(wide_s)
    wide_s[0:block, :] = resid.astype(F32)
    send = jnp.dot(select_ref[...], wide_s[...].astype(BF16), preferred_element_type=F32)
    for e in range(send_ref.shape[0]):
        own = send[e * MOST : (e + 1) * MOST]
        rows = [own[:, 0:384], own[:, 384:768]]
        rows.append(jnp.concatenate([own[0:1, 768:], own[2:3, 768:896]], 1))
        rows.append(jnp.concatenate([own[1:2, 768:], own[2:3, 896:]], 1))
        send_ref[e] = jnp.concatenate(rows, 0).astype(BF16)


def slots_kernel(got_ref, _0, out_ref, slots_s):
    for j in range(got_ref.shape[0]):
        own = got_ref[j].astype(F32)
        at = j * MOST
        slots_s[at : at + 3, 0:384] = own[0:3]
        slots_s[at : at + 3, 384:768] = own[3:6]
        slots_s[at : at + 1, 768:] = own[6:7, 0:256]
        slots_s[at + 1 : at + 2, 768:] = own[7:8, 0:256]
        slots_s[at + 2 : at + 3, 768:] = jnp.concatenate([own[6:7, 256:], own[7:8, 256:]], 1)
    out_ref[...] = slots_s[...].astype(BF16)


def stage_kernel(w0_ref, w1_ref, w2_ref, w3_ref, out_ref, sems):
    hidden = w1_ref.shape[1]
    copies = []
    for d, w_ref in enumerate((w0_ref, w1_ref, w2_ref, w3_ref)):
        copies.append(pltpu.make_async_copy(w_ref, out_ref.at[:, pl.ds(d * hidden, hidden)], sems.at[d]))
        copies[d].start()
    for copy in copies:
        copy.wait()


def expert_kernel(me_ref, tok_ref, gain_ref, resid_ref, w_ref, out_ref):
    me = me_ref[0]
    slots, cols = tok_ref.shape
    quarters = out_ref.shape[0]
    hidden = w_ref.shape[1] // quarters
    tok = tok_ref[...].astype(F32)
    sums = jnp.sum(tok * tok, axis=-1, keepdims=True)
    sums = jnp.broadcast_to(sums, (slots, 128)).T[0:MOST]
    first = sums.astype(BF16).astype(F32)
    second = (sums - first).astype(BF16).astype(F32)
    third = sums - first - second
    row = lax.broadcasted_iota(jnp.int32, (MOST, slots), 0)
    scales = jnp.where(row == 0, first, jnp.where(row == 1, second, third))
    resid = resid_ref[...].astype(F32)
    rows = resid.shape[0] // quarters
    for h in range(quarters):
        pieces = [scales]
        for r in range(rows):
            own = resid[h * rows + r : h * rows + r + 1, :]
            pieces.append(own[:, 0:hidden])
            pieces.append(own[:, hidden : 2 * hidden])
            pieces.append(jnp.concatenate([own[:, 2 * hidden :], jnp.zeros((1, 3 * hidden - cols), F32)], 1))
        pieces.append(jnp.zeros((16 - 4 * MOST, hidden), F32))
        out_ref[h, slots:, :] = jnp.concatenate(pieces, 0).astype(BF16)
    tok = (tok * gain_ref[...]).astype(BF16)
    for d in range(0, quarters, 2):
        pair = jnp.dot(tok, w_ref[:, d * hidden : (d + 2) * hidden], preferred_element_type=F32).astype(BF16)
        for i in range(2):
            out_ref[lax.rem(me - d - i + quarters, quarters), 0:slots, :] = pair[:, i * hidden : (i + 1) * hidden]


def finish_kernel(part_ref, wts_ref, out_ref, resid_ref, resid_s):
    quarters, _, hidden = part_ref.shape
    slots = out_ref.shape[0]
    rows, width = resid_ref.shape
    cols = width // quarters
    total = jnp.zeros((slots, hidden), F32)
    squares = jnp.zeros((1, slots), F32)
    for q in range(quarters):
        total = total + part_ref[q, 0:slots, :].astype(F32)
        own = part_ref[q, slots:, :].astype(F32)
        squares = squares + (own[0:1] + own[1:2] + own[2:3])
        for r in range(rows):
            for m in range(3):
                size = min(hidden, cols - m * hidden)
                at = q * cols + m * hidden
                resid_s[r : r + 1, at : at + size] = own[3 + 3 * r + m : 4 + 3 * r + m, 0:size]
    resid_ref[...] = resid_s[0:rows, :].astype(BF16)
    row = lax.broadcasted_iota(jnp.int32, (8, slots), 0)
    scale = lax.rsqrt(squares / width + 1e-05)
    both = jnp.where(row == 0, scale, wts_ref[...]).T
    out_ref[...] = (silu(total * both[:, 0:1]) * both[:, 1:2]).astype(BF16)


def shards(
    x_in,
    norm_gain,
    w_in_x,
    w_in_z,
    conv_weight,
    conv_bias,
    w_xproj,
    w_dt,
    dt_bias,
    a_log,
    d_skip,
    w_out,
    moe_gain,
    route_ids,
    route_weights,
    w_gate,
):
    n_seq, n_exp, n_hid = (lax.axis_size(a) for a in ("seq", "exp", "hid"))
    at_seq, at_exp, at_hid = (lax.axis_index(a) for a in ("seq", "exp", "hid"))
    rows, width = x_in.shape
    tokens = rows * n_exp * n_hid
    channels = w_in_x.shape[1]
    states = a_log.shape[0]
    rank = w_dt.shape[0]
    block = rows * n_hid
    cols = width // n_hid
    per = n_seq // n_hid

    w_x = lax.all_gather(w_in_x, "seq", axis=0, tiled=True)

    own_routes = jnp.concatenate([route_ids.astype(BF16), route_weights], 1)
    own = jnp.concatenate([x_in, jnp.pad(own_routes, ((0, 0), (0, 124)))], 1)
    over_exp = lax.all_gather(own, "exp", axis=0, tiled=False)
    quarter_rows = call(
        rows_kernel,
        "rows",
        like((n_hid, n_exp * rows, width + 128), BF16),
        [(n_exp * rows, width + 128)],
        over_exp,
    )
    quarter_rows, w_out, w_in_z = lax.optimization_barrier((quarter_rows, w_out, w_in_z))
    w_z = lax.all_gather(w_in_z, "seq", axis=0, tiled=True)
    route = [
        (s * n_hid + h, (h * per + s % per) * n_hid + s // per) for s in range(n_seq) for h in range(n_hid)
    ]
    w_out_here = lax.ppermute(w_out, ("seq", "hid"), route)
    w_out_all = lax.all_gather(w_out_here, "seq", axis=0, tiled=False)
    params = jnp.concatenate(
        [a_log, conv_weight, conv_bias[None], dt_bias[None], d_skip[None], jnp.zeros((1, channels), F32)], 0
    )
    all_rows = exchange(quarter_rows, "hid")
    x_block = lax.dynamic_slice(
        all_rows.reshape(n_hid, n_exp, rows, -1), (0, at_exp, 0, at_hid * cols), (n_hid, 1, rows, cols)
    ).reshape(block, cols)
    stream, tail, routes = call(
        project_kernel,
        "project",
        (like((tokens, channels), BF16), like((8, channels), F32), like((tokens, 128), F32)),
        [(tokens, channels), (tokens, 128), (tokens, channels)],
        all_rows,
        norm_gain[None],
        near(w_x, "near_x"),
    )
    gate_in = call(
        project_gate_kernel,
        "project_gate",
        like((tokens, channels), BF16),
        [(tokens, channels), (tokens, channels)],
        all_rows,
        norm_gain[None],
        w_z,
    )
    halo = lax.ppermute(tail, "seq", [(i, i + 1) for i in range(n_seq - 1)])
    inner_act, tiles = call(
        conv_kernel,
        "conv",
        (like((tokens, channels), BF16), like((n_exp * n_hid, 8, 128), BF16)),
        [(tokens + 8, channels)],
        stream,
        halo,
        params,
        w_xproj,
    )

    got = exchange(tiles, ("exp", "hid"))
    back = exchange(call(tile_sum_kernel, "tile_sum", like(got.shape, BF16), [], got), ("exp", "hid"))

    rows_ids = routes[:, :2].reshape(n_exp, -1)
    rows_wts = routes[:, 2:4].reshape(n_exp, -1)
    n_rows = rows_ids.shape[1]
    upto = (jnp.arange(n_rows)[:, None] <= jnp.arange(n_rows)[None, :]).astype(F32)
    named = (rows_ids == at_exp.astype(F32)).astype(F32)
    place = jnp.dot(named, upto) * named
    slot_wts = jnp.stack(
        [jnp.sum(jnp.where(place == i + 1.0, rows_wts, 0.0), 1) for i in range(MOST)], 1
    ).reshape(1, -1)
    n_slots = slot_wts.shape[1]
    ids = lax.dynamic_index_in_dim(rows_ids, at_exp, 0, keepdims=False)
    onehot = (ids[:, None] == jnp.arange(n_exp, dtype=F32)[None, :]).astype(F32)
    position = jnp.sum(jnp.dot(upto.T, onehot) * onehot, 1) - 1.0
    target = ids * MOST + position
    select = (target[None, :] == jnp.arange(n_exp * MOST, dtype=F32)[:, None]).astype(F32)
    select = jnp.sum(select.reshape(n_exp * MOST, block, -1), 2)
    select = jnp.pad(select, ((0, 0), (0, 16 - block))).astype(BF16)

    def pick(w, d):
        return lax.dynamic_index_in_dim(w[0].reshape(n_hid, cols, -1), (at_hid + d) % n_hid, 0, keepdims=False)

    def shift(w, d):
        return lax.ppermute(pick(w, d), "hid", [(i, (i + d) % n_hid) for i in range(n_hid)])

    slot_wts, w_first = lax.optimization_barrier((slot_wts, w_gate))
    w_2 = shift(w_first, 2)
    local, carried = call(
        scan_kernel,
        "scan",
        (
            like((2 * tokens + 2 * states, channels), F32),
            like((n_seq, states + 8, channels), F32),
        ),
        [(tokens, rank), (tokens, channels), (tokens, channels)],
        back,
        w_dt,
        params,
        inner_act,
        jnp.pad(slot_wts, ((0, 0), (0, channels - n_slots))),
    )
    carried_all = exchange(carried, "seq")
    weights = carried_all[:, states + 1, :n_slots].reshape(1, -1)
    gated = call(
        gate_kernel,
        "gate",
        like((n_hid, tokens, channels), BF16),
        [(tokens, channels)],
        at_seq.astype(jnp.int32)[None],
        carried_all,
        params,
        local,
        gate_in,
        scalars=1,
    )

    gated_all = exchange(gated, "hid")
    mixed = call(
        mix_kernel,
        "mix",
        like((n_exp, 8, block * cols // 8), BF16),
        [(tokens, cols)],
        gated_all,
        near(w_out_all, "near_out"),
        w_2,
        unread=1,
    )
    mixed, w_second = lax.optimization_barrier((mixed, w_gate))
    w_own, w_1, w_3 = pick(w_second, 0), shift(w_second, 1), shift(w_second, 3)
    sums = exchange(mixed, "exp")
    resid_part, send = call(
        resid_kernel,
        "resid",
        (like((block, cols), BF16), like((n_exp, 8, MOST * cols // 8), BF16)),
        [(16, cols)],
        sums,
        x_block,
        select,
    )

    hidden = w_gate.shape[2]
    w_side = call(
        stage_kernel,
        "stage",
        like((cols, n_hid * hidden), BF16),
        [],
        w_own,
        w_1,
        w_2,
        w_3,
        unread=4,
        more=[pltpu.SemaphoreType.DMA((n_hid,))],
    )
    slots = call(
        slots_kernel,
        "slots",
        like((n_exp * MOST, cols), BF16),
        [(n_exp * MOST, cols)],
        exchange(send, "exp"),
        w_side,
        unread=1,
    )
    all_slots = lax.all_gather(slots, "seq", axis=0, tiled=True)
    n_all = all_slots.shape[0]
    away = call(
        expert_kernel,
        "expert",
        like((n_hid, n_all + 16, hidden), BF16),
        [],
        at_hid.astype(jnp.int32)[None],
        all_slots,
        lax.dynamic_slice_in_dim(moe_gain, at_hid * cols, cols, 0)[None],
        resid_part,
        w_side,
        scalars=1,
    )
    home = exchange(away, "hid")
    activated, resid = call(
        finish_kernel,
        "finish",
        (like((n_all, hidden), BF16), like((rows, width), BF16)),
        [(8, width)],
        home,
        weights,
    )
    return (resid, activated[None])


def solution(mesh):
    in_specs = (
        P(("seq", "exp", "hid"), None),
        P(),
        P("seq", ("exp", "hid")),
        P("seq", ("exp", "hid")),
        P(None, ("exp", "hid")),
        P(("exp", "hid")),
        P(("exp", "hid"), None),
        P(None, ("exp", "hid")),
        P(("exp", "hid")),
        P(None, ("exp", "hid")),
        P(("exp", "hid")),
        P(("exp", "hid"), "seq"),
        P(),
        P(("seq", "exp", "hid"), None),
        P(("seq", "exp", "hid"), None),
        P("exp", None, ("seq", "hid")),
    )
    out_specs = (P(("seq", "exp", "hid"), None), P("exp", None, ("seq", "hid")))
    return jax.shard_map(shards, mesh=mesh, in_specs=in_specs, out_specs=out_specs, check_vma=False)
```

```python
import jax
import jax.numpy as jnp
from jax import lax
from jax.experimental import pallas as pl
from jax.experimental.pallas import tpu as pltpu
from jax.sharding import PartitionSpec as P

F32 = jnp.float32
BF16 = jnp.bfloat16
MOST = 3
STATES = 16
CONV = 4
TAPS, BIAS, STEP, SKIP = 16, 20, 21, 22


def exchange(x, axis):
    return lax.all_to_all(x, axis, split_axis=0, concat_axis=0, tiled=True)


def softplus(v):
    return jnp.maximum(v, 0.0) + jnp.log1p(jnp.exp(-jnp.abs(v)))


def silu(v):
    return v / (1.0 + jnp.exp(-v))


def call(body, name, out_shape, scratch, *args, scalars=0, unread=0, more=(), limit=40):
    vmem, smem = pl.BlockSpec(memory_space=pltpu.VMEM), pl.BlockSpec(memory_space=pltpu.SMEM)
    return pl.pallas_call(
        body,
        out_shape=out_shape,
        in_specs=[smem] * scalars
        + [vmem] * (len(args) - scalars - unread)
        + [pl.BlockSpec(memory_space=pl.ANY)] * unread,
        out_specs=jax.tree.map(lambda _: vmem, out_shape),
        scratch_shapes=[pltpu.VMEM(shape, F32) for shape in scratch] + list(more),
        compiler_params=pltpu.CompilerParams(vmem_limit_bytes=limit * 2**20),
        name=name,
    )(*args)


def near_kernel(x_ref, out_ref, sem):
    copy = pltpu.make_async_copy(x_ref, out_ref, sem)
    copy.start()
    copy.wait()


def near(x, name):
    return call(near_kernel, name, like(x.shape, x.dtype), [], x, unread=1, more=[pltpu.SemaphoreType.DMA])


def like(shape, dtype):
    return jax.ShapeDtypeStruct(shape, dtype)


def rows_kernel(x_ref, out_ref, rows_s):
    groups, rows, width = x_ref.shape
    for g in range(groups):
        rows_s[g * rows : (g + 1) * rows, :] = x_ref[g].astype(F32)
    x = rows_s[...]
    scale = lax.rsqrt(jnp.mean(x * x, axis=-1, keepdims=True) + 1e-05)
    first = scale.astype(BF16).astype(F32)
    second = (scale - first).astype(BF16).astype(F32)
    lane = lax.broadcasted_iota(jnp.int32, (groups * rows, 128), 1)
    more = jnp.zeros((groups * rows, 128), F32)
    for at, value in enumerate((first, second, scale - first - second)):
        more = jnp.where(lane == at, value, more)
    for h in range(out_ref.shape[0]):
        out_ref[h, :, 0:width] = x.astype(BF16)
        out_ref[h, :, width:] = more.astype(BF16)


def normed_rows(x_ref, gain_ref, width):
    normed = []
    for h in range(x_ref.shape[0]):
        more = x_ref[h, :, width:].astype(F32)
        scale = more[:, 0:1] + more[:, 1:2] + more[:, 2:3]
        normed.append((x_ref[h, :, 0:width].astype(F32) * scale * gain_ref[...]).astype(BF16))
    return jnp.concatenate(normed, 0)


def in_order(source, target, quarters):
    part = source.shape[0] // quarters
    groups = part // MOST
    for h in range(quarters):
        for r in range(MOST):
            own = source[pl.ds(h * part + r, groups, stride=MOST), :]
            target[pl.ds(h * MOST + r, groups, stride=quarters * MOST), :] = own


def project_kernel(x_ref, gain_ref, w_ref, stream_ref, tail_ref, mixed_s, stream_s):
    quarters, part, _ = x_ref.shape
    normed = normed_rows(x_ref, gain_ref, w_ref.shape[0])
    mixed_s[...] = jnp.dot(normed, w_ref[...], preferred_element_type=F32)
    in_order(mixed_s, stream_s, quarters)
    stream_ref[...] = stream_s[...].astype(BF16)
    tail_ref[...] = stream_s[quarters * part - 8 :, :].astype(BF16).astype(F32)


def project_gate_kernel(x_ref, gain_ref, w_ref, gate_ref, mixed_s, gate_s):
    normed = normed_rows(x_ref, gain_ref, w_ref.shape[0])
    mixed_s[...] = jnp.dot(normed, w_ref[...], preferred_element_type=F32)
    in_order(mixed_s, gate_s, x_ref.shape[0])
    gate_ref[...] = gate_s[...].astype(BF16)


def conv_kernel(stream_ref, halo_ref, params_ref, wx_ref, act_ref, tile_ref, pad_s, wide_s, tile_s):
    tokens, channels = stream_ref.shape
    pad_s[0:8, :] = halo_ref[...]
    pad_s[8:, :] = stream_ref[...].astype(F32)
    conv = params_ref[BIAS : BIAS + 1, :] + jnp.zeros((tokens, channels), F32)
    for k in range(CONV):
        at = 8 - (CONV - 1) + k
        conv = conv + params_ref[TAPS + k : TAPS + k + 1, :] * pad_s[at : at + tokens, :]
    act = silu(conv).astype(BF16)
    act_ref[...] = act
    wide = jnp.dot(act, wx_ref[...], preferred_element_type=F32)
    blocks = wide_s.shape[0]
    for i in range(blocks):
        wide_s[i] = wide[:, i * 128 : i * 128 + 128]
    groups = tile_ref.shape[0]
    maps = jnp.zeros((groups, 128), F32)
    for r in range(MOST):
        own = pl.ds(r, groups, stride=MOST)
        for c in range(2):
            tile_s[pl.ds(2 * r + c, groups, stride=8), :] = wide_s[c, own, :]
        maps = maps + wide_s[2 + r, own, :]
    tile_s[pl.ds(6, groups, stride=8), :] = maps
    tile_s[pl.ds(7, groups, stride=8), :] = jnp.zeros((groups, 128), F32)
    tile_ref[...] = tile_s[...].reshape(groups, 8, 128).astype(BF16)


def tile_sum_kernel(got_ref, route_ref, _0, out_ref):
    total = jnp.sum(got_ref[...].astype(F32), axis=0)
    row = lax.broadcasted_iota(jnp.int32, total.shape, 0)
    total = jnp.where(row == 7, route_ref[...], total).astype(BF16)
    out_ref[...] = jnp.broadcast_to(total[None], out_ref.shape)


def scan_kernel(back_ref, wdt_ref, params_ref, act_ref, out_ref, send_ref, tile_s, low_s, step_s, drive_s):
    _, tokens, half = low_s.shape
    groups = back_ref.shape[0]
    tile_s[...] = back_ref[...].astype(F32).reshape(groups * 8, 128)
    for r in range(MOST):
        for c in range(2):
            low_s[c, pl.ds(r, groups, stride=MOST), :] = tile_s[pl.ds(2 * r + c, groups, stride=8), :]
    blank = jnp.zeros((128 - groups, 128), F32)
    maps = jnp.concatenate([tile_s[pl.ds(6, groups, stride=8), :], blank], 0).T
    routes = jnp.concatenate([tile_s[pl.ds(7, groups, stride=8), :], blank], 0).T
    out_ref[2 * tokens :, :] = maps
    decay = -jnp.exp(params_ref[0:STATES, :])
    states, channels = decay.shape
    step = jnp.dot(low_s[0].astype(BF16), wdt_ref[0:half, :], preferred_element_type=F32)
    step = step + jnp.dot(low_s[1].astype(BF16), wdt_ref[half:, :], preferred_element_type=F32)
    step = softplus(step + params_ref[STEP : STEP + 1, :])
    step_s[...] = step
    act = act_ref[...].astype(F32)
    drive_s[...] = step * act
    state = jnp.zeros((states, channels), F32)
    total = jnp.zeros((1, channels), F32)
    for t in range(tokens):
        at, own = t % MOST * 32, t // MOST
        step_t = step_s[t : t + 1, :]
        b_t = jnp.broadcast_to(maps[at : at + 16, own : own + 1], (states, channels))
        c_t = jnp.broadcast_to(maps[at + 16 : at + 32, own : own + 1], (states, channels))
        state = jnp.exp(step_t * decay) * state + drive_s[t : t + 1, :] * b_t
        total = total + step_t
        out_ref[t : t + 1, :] = jnp.sum(c_t * state, axis=0, keepdims=True)
        out_ref[tokens + t : tokens + t + 1, :] = total
    out_ref[0:tokens, :] = out_ref[0:tokens, :] + params_ref[SKIP : SKIP + 1, :] * act
    routes = jnp.concatenate([routes[0:6, 0:groups], routes[6:12, 0:groups]], 1)
    tail = jnp.concatenate([total, routes, jnp.zeros((1, channels), F32)], 0)
    for k in range(send_ref.shape[0]):
        send_ref[k, 0:states, :] = state
        send_ref[k, states:, :] = tail


def gate_kernel(me_ref, all_ref, params_ref, local_ref, z_ref, out_ref, corr_s):
    tokens = z_ref.shape[0]
    decay = -jnp.exp(params_ref[0:STATES, :])
    states, channels = decay.shape
    state = jnp.zeros((states, channels), F32)
    me = me_ref[0]
    for k in range(all_ref.shape[0] - 1):
        total = all_ref[k, states : states + 1, :]
        later = jnp.exp(total * decay) * state + all_ref[k, 0:states, :]
        state = jnp.where(k < me, later, state)
    maps = local_ref[2 * tokens :, :]
    for t in range(tokens):
        at, own = t % MOST * 32 + 16, t // MOST
        c_t = jnp.broadcast_to(maps[at : at + 16, own : own + 1], (states, channels))
        term = c_t * (jnp.exp(local_ref[tokens + t : tokens + t + 1, :] * decay) * state)
        corr_s[t : t + 1, :] = jnp.sum(term, axis=0, keepdims=True)
    z = z_ref[...].astype(F32)
    ssm = local_ref[0:tokens, :] + corr_s[...]
    gated = (ssm * silu(z)).astype(BF16)
    for h in range(out_ref.shape[0]):
        out_ref[h] = gated


def mix_kernel(gated_ref, w_ref, _0, out_ref, mixed_s):
    quarters = gated_ref.shape[0]
    per = w_ref.shape[0] // quarters
    cols = w_ref.shape[2]
    for b in range(per):
        total = jnp.dot(gated_ref[0], w_ref[b], preferred_element_type=F32)
        for h in range(1, quarters):
            total = total + jnp.dot(gated_ref[h], w_ref[h * per + b], preferred_element_type=F32)
        mixed_s[:, b * cols : (b + 1) * cols] = total
    block = mixed_s.shape[0] // out_ref.shape[0]
    wide = mixed_s.shape[1]
    for j in range(out_ref.shape[0]):
        own = mixed_s[j * block : (j + 1) * block, :]
        rest = jnp.concatenate([own[8:, : wide // 2], own[8:, wide // 2 :]], 0)
        out_ref[j] = jnp.concatenate([own[:8], rest], 1).astype(BF16)


def resid_kernel(parts_ref, x_ref, select_ref, resid_ref, send_ref, wide_s):
    block, cols = resid_ref.shape
    sums = jnp.sum(parts_ref[...].astype(F32), axis=0)
    rest = jnp.concatenate([sums[: block - 8, cols:], sums[block - 8 :, cols:]], 1)
    total = x_ref[...].astype(F32) + jnp.concatenate([sums[:, :cols], rest], 0)
    resid = total.astype(BF16)
    resid_ref[...] = resid
    wide_s[...] = jnp.zeros_like(wide_s)
    wide_s[0:block, :] = resid.astype(F32)
    send = jnp.dot(select_ref[...], wide_s[...].astype(BF16), preferred_element_type=F32)
    for e in range(send_ref.shape[0]):
        own = send[e * MOST : (e + 1) * MOST]
        rows = [own[:, 0:384], own[:, 384:768]]
        rows.append(jnp.concatenate([own[0:1, 768:], own[2:3, 768:896]], 1))
        rows.append(jnp.concatenate([own[1:2, 768:], own[2:3, 896:]], 1))
        send_ref[e] = jnp.concatenate(rows, 0).astype(BF16)


def slots_kernel(got_ref, _0, out_ref, slots_s):
    for j in range(got_ref.shape[0]):
        own = got_ref[j].astype(F32)
        at = j * MOST
        slots_s[at : at + 3, 0:384] = own[0:3]
        slots_s[at : at + 3, 384:768] = own[3:6]
        slots_s[at : at + 1, 768:] = own[6:7, 0:256]
        slots_s[at + 1 : at + 2, 768:] = own[7:8, 0:256]
        slots_s[at + 2 : at + 3, 768:] = jnp.concatenate([own[6:7, 256:], own[7:8, 256:]], 1)
    out_ref[...] = slots_s[...].astype(BF16)


def stage_kernel(w0_ref, w1_ref, w2_ref, w3_ref, out_ref, sems):
    hidden = w1_ref.shape[1]
    copies = []
    for d, w_ref in enumerate((w0_ref, w1_ref, w2_ref, w3_ref)):
        copies.append(pltpu.make_async_copy(w_ref, out_ref.at[:, pl.ds(d * hidden, hidden)], sems.at[d]))
        copies[d].start()
    for copy in copies:
        copy.wait()


def expert_kernel(me_ref, tok_ref, gain_ref, resid_ref, w_ref, out_ref):
    me = me_ref[0]
    slots, cols = tok_ref.shape
    quarters = out_ref.shape[0]
    hidden = w_ref.shape[1] // quarters
    tok = tok_ref[...].astype(F32)
    sums = jnp.sum(tok * tok, axis=-1, keepdims=True)
    sums = jnp.broadcast_to(sums, (slots, 128)).T[0:MOST]
    first = sums.astype(BF16).astype(F32)
    second = (sums - first).astype(BF16).astype(F32)
    third = sums - first - second
    row = lax.broadcasted_iota(jnp.int32, (MOST, slots), 0)
    scales = jnp.where(row == 0, first, jnp.where(row == 1, second, third))
    resid = resid_ref[...].astype(F32)
    rows = resid.shape[0] // quarters
    for h in range(quarters):
        pieces = [scales]
        for r in range(rows):
            own = resid[h * rows + r : h * rows + r + 1, :]
            pieces.append(own[:, 0:hidden])
            pieces.append(own[:, hidden : 2 * hidden])
            pieces.append(jnp.concatenate([own[:, 2 * hidden :], jnp.zeros((1, 3 * hidden - cols), F32)], 1))
        pieces.append(jnp.zeros((16 - 4 * MOST, hidden), F32))
        out_ref[h, slots:, :] = jnp.concatenate(pieces, 0).astype(BF16)
    tok = (tok * gain_ref[...]).astype(BF16)
    for d in range(0, quarters, 2):
        pair = jnp.dot(tok, w_ref[:, d * hidden : (d + 2) * hidden], preferred_element_type=F32).astype(BF16)
        for i in range(2):
            out_ref[lax.rem(me - d - i + quarters, quarters), 0:slots, :] = pair[:, i * hidden : (i + 1) * hidden]


def finish_kernel(part_ref, wts_ref, out_ref, resid_ref, resid_s):
    quarters, _, hidden = part_ref.shape
    slots = out_ref.shape[0]
    rows, width = resid_ref.shape
    cols = width // quarters
    total = jnp.zeros((slots, hidden), F32)
    squares = jnp.zeros((1, slots), F32)
    for q in range(quarters):
        total = total + part_ref[q, 0:slots, :].astype(F32)
        own = part_ref[q, slots:, :].astype(F32)
        squares = squares + (own[0:1] + own[1:2] + own[2:3])
        for r in range(rows):
            for m in range(3):
                size = min(hidden, cols - m * hidden)
                at = q * cols + m * hidden
                resid_s[r : r + 1, at : at + size] = own[3 + 3 * r + m : 4 + 3 * r + m, 0:size]
    resid_ref[...] = resid_s[0:rows, :].astype(BF16)
    row = lax.broadcasted_iota(jnp.int32, (8, slots), 0)
    scale = lax.rsqrt(squares / width + 1e-05)
    both = jnp.where(row == 0, scale, wts_ref[...]).T
    out_ref[...] = (silu(total * both[:, 0:1]) * both[:, 1:2]).astype(BF16)


def shards(
    x_in,
    norm_gain,
    w_in_x,
    w_in_z,
    conv_weight,
    conv_bias,
    w_xproj,
    w_dt,
    dt_bias,
    a_log,
    d_skip,
    w_out,
    moe_gain,
    route_ids,
    route_weights,
    w_gate,
):
    n_seq, n_exp, n_hid = (lax.axis_size(a) for a in ("seq", "exp", "hid"))
    at_seq, at_exp, at_hid = (lax.axis_index(a) for a in ("seq", "exp", "hid"))
    rows, width = x_in.shape
    tokens = rows * n_exp * n_hid
    channels = w_in_x.shape[1]
    states = a_log.shape[0]
    rank = w_dt.shape[0]
    block = rows * n_hid
    cols = width // n_hid
    per = n_seq // n_hid

    w_x = lax.all_gather(w_in_x, "seq", axis=0, tiled=True)

    over_exp = lax.all_gather(x_in, "exp", axis=0, tiled=False)
    quarter_rows = call(
        rows_kernel,
        "rows",
        like((n_hid, n_exp * rows, width + 128), BF16),
        [(n_exp * rows, width)],
        over_exp,
    )
    quarter_rows, w_out, w_in_z = lax.optimization_barrier((quarter_rows, w_out, w_in_z))
    w_z = lax.all_gather(w_in_z, "seq", axis=0, tiled=True)
    route = [
        (s * n_hid + h, (h * per + s % per) * n_hid + s // per) for s in range(n_seq) for h in range(n_hid)
    ]
    w_out_here = lax.ppermute(w_out, ("seq", "hid"), route)
    w_out_all = lax.all_gather(w_out_here, "seq", axis=0, tiled=False)
    w_maps = w_xproj[:, rank:]
    w_maps = jnp.concatenate(
        [w_xproj[:, :rank]] + [jnp.pad(w_maps, ((0, 0), (32 * r, 96 - 32 * r))) for r in range(rows)], 1
    )
    routes = jnp.concatenate([route_ids.astype(F32), route_weights.astype(F32)], 1).T.reshape(1, -1)
    routes = jnp.pad(routes, ((0, 0), (0, 128 - routes.shape[1])))
    params = jnp.concatenate(
        [a_log, conv_weight, conv_bias[None], dt_bias[None], d_skip[None], jnp.zeros((1, channels), F32)], 0
    )
    all_rows = exchange(quarter_rows, "hid")
    x_block = lax.dynamic_slice(
        all_rows.reshape(n_hid, n_exp, rows, -1), (0, at_exp, 0, at_hid * cols), (n_hid, 1, rows, cols)
    ).reshape(block, cols)
    stream, tail = call(
        project_kernel,
        "project",
        (like((tokens, channels), BF16), like((8, channels), F32)),
        [(tokens, channels), (tokens, channels)],
        all_rows,
        norm_gain[None],
        near(w_x, "near_x"),
    )
    gate_in = call(
        project_gate_kernel,
        "project_gate",
        like((tokens, channels), BF16),
        [(tokens, channels), (tokens, channels)],
        all_rows,
        norm_gain[None],
        w_z,
    )
    halo = lax.ppermute(tail, "seq", [(i, i + 1) for i in range(n_seq - 1)])
    inner_act, tiles = call(
        conv_kernel,
        "conv",
        (like((tokens, channels), BF16), like((n_exp * n_hid, 8, 128), BF16)),
        [(tokens + 8, channels), (5, tokens, 128), (n_exp * n_hid * 8, 128)],
        stream,
        halo,
        params,
        w_maps,
    )

    got = exchange(tiles, ("exp", "hid"))
    back = exchange(call(tile_sum_kernel, "tile_sum", like(got.shape, BF16), [], got, routes, gate_in, unread=1), ("exp", "hid"))

    def pick(w, d):
        return lax.dynamic_index_in_dim(w[0].reshape(n_hid, cols, -1), (at_hid + d) % n_hid, 0, keepdims=False)

    def shift(w, d):
        return lax.ppermute(pick(w, d), "hid", [(i, (i + d) % n_hid) for i in range(n_hid)])

    gate_in, w_first = lax.optimization_barrier((gate_in, w_gate))
    w_2 = shift(w_first, 2)
    local, carried = call(
        scan_kernel,
        "scan",
        (
            like((2 * tokens + 128, channels), F32),
            like((n_seq, states + 8, channels), F32),
        ),
        [(n_exp * n_hid * 8, 128), (2, tokens, 128), (tokens, channels), (tokens, channels)],
        back,
        w_dt,
        params,
        inner_act,
    )
    carried_all = exchange(carried, "seq")

    routed = carried_all[:, states + 1 : states + 7].reshape(n_seq, 6, 2, -1).transpose(0, 2, 1, 3)
    routed = routed.reshape(n_seq, 4, rows, -1).transpose(0, 3, 2, 1).reshape(n_seq * n_exp, block, 4)
    rows_ids = routed[:, :, :2].reshape(n_seq * n_exp, -1)
    rows_wts = routed[:, :, 2:].reshape(n_seq * n_exp, -1)
    n_rows = rows_ids.shape[1]
    upto = (jnp.arange(n_rows)[:, None] <= jnp.arange(n_rows)[None, :]).astype(F32)
    named = (rows_ids == at_exp.astype(F32)).astype(F32)
    place = jnp.dot(named, upto) * named
    weights = jnp.stack(
        [jnp.sum(jnp.where(place == i + 1.0, rows_wts, 0.0), 1) for i in range(MOST)], 1
    ).reshape(1, -1)
    ids = lax.dynamic_index_in_dim(rows_ids, at_seq * n_exp + at_exp, 0, keepdims=False)
    onehot = (ids[:, None] == jnp.arange(n_exp, dtype=F32)[None, :]).astype(F32)
    position = jnp.sum(jnp.dot(upto.T, onehot) * onehot, 1) - 1.0
    target = ids * MOST + position
    select = (target[None, :] == jnp.arange(n_exp * MOST, dtype=F32)[:, None]).astype(F32)
    select = jnp.sum(select.reshape(n_exp * MOST, block, -1), 2)
    select = jnp.pad(select, ((0, 0), (0, 16 - block))).astype(BF16)
    gated = call(
        gate_kernel,
        "gate",
        like((n_hid, tokens, channels), BF16),
        [(tokens, channels)],
        at_seq.astype(jnp.int32)[None],
        carried_all,
        params,
        local,
        gate_in,
        scalars=1,
    )

    gated_all = exchange(gated, "hid")
    mixed = call(
        mix_kernel,
        "mix",
        like((n_exp, 8, block * cols // 8), BF16),
        [(tokens, cols)],
        gated_all,
        near(w_out_all, "near_out"),
        w_2,
        unread=1,
    )
    mixed, w_second = lax.optimization_barrier((mixed, w_gate))
    w_own, w_1, w_3 = pick(w_second, 0), shift(w_second, 1), shift(w_second, 3)
    sums = exchange(mixed, "exp")
    resid_part, send = call(
        resid_kernel,
        "resid",
        (like((block, cols), BF16), like((n_exp, 8, MOST * cols // 8), BF16)),
        [(16, cols)],
        sums,
        x_block,
        select,
    )

    hidden = w_gate.shape[2]
    w_side = call(
        stage_kernel,
        "stage",
        like((cols, n_hid * hidden), BF16),
        [],
        w_own,
        w_1,
        w_2,
        w_3,
        unread=4,
        more=[pltpu.SemaphoreType.DMA((n_hid,))],
    )
    slots = call(
        slots_kernel,
        "slots",
        like((n_exp * MOST, cols), BF16),
        [(n_exp * MOST, cols)],
        exchange(send, "exp"),
        w_side,
        unread=1,
    )
    all_slots = lax.all_gather(slots, "seq", axis=0, tiled=True)
    n_all = all_slots.shape[0]
    away = call(
        expert_kernel,
        "expert",
        like((n_hid, n_all + 16, hidden), BF16),
        [],
        at_hid.astype(jnp.int32)[None],
        all_slots,
        lax.dynamic_slice_in_dim(moe_gain, at_hid * cols, cols, 0)[None],
        resid_part,
        w_side,
        scalars=1,
    )
    home = exchange(away, "hid")
    activated, resid = call(
        finish_kernel,
        "finish",
        (like((n_all, hidden), BF16), like((rows, width), BF16)),
        [(8, width)],
        home,
        weights,
    )
    return (resid, activated[None])


def solution(mesh):
    in_specs = (
        P(("seq", "exp", "hid"), None),
        P(),
        P("seq", ("exp", "hid")),
        P("seq", ("exp", "hid")),
        P(None, ("exp", "hid")),
        P(("exp", "hid")),
        P(("exp", "hid"), None),
        P(None, ("exp", "hid")),
        P(("exp", "hid")),
        P(None, ("exp", "hid")),
        P(("exp", "hid")),
        P(("exp", "hid"), "seq"),
        P(),
        P(("seq", "exp", "hid"), None),
        P(("seq", "exp", "hid"), None),
        P("exp", None, ("seq", "hid")),
    )
    out_specs = (P(("seq", "exp", "hid"), None), P("exp", None, ("seq", "hid")))
    return jax.shard_map(shards, mesh=mesh, in_specs=in_specs, out_specs=out_specs, check_vma=False)
```

```python
import jax
import jax.numpy as jnp
from jax import lax
from jax.experimental import pallas as pl
from jax.experimental.pallas import tpu as pltpu
from jax.sharding import PartitionSpec as P

F32 = jnp.float32
BF16 = jnp.bfloat16
MOST = 3
STATES = 16
CONV = 4
TAPS, BIAS, STEP, SKIP = 16, 20, 21, 22


def exchange(x, axis):
    return lax.all_to_all(x, axis, split_axis=0, concat_axis=0, tiled=True)


def softplus(v):
    return jnp.maximum(v, 0.0) + jnp.log1p(jnp.exp(-jnp.abs(v)))


def silu(v):
    return v / (1.0 + jnp.exp(-v))


def call(body, name, out_shape, scratch, *args, scalars=0, unread=0, more=(), limit=40):
    vmem, smem = pl.BlockSpec(memory_space=pltpu.VMEM), pl.BlockSpec(memory_space=pltpu.SMEM)
    return pl.pallas_call(
        body,
        out_shape=out_shape,
        in_specs=[smem] * scalars
        + [vmem] * (len(args) - scalars - unread)
        + [pl.BlockSpec(memory_space=pl.ANY)] * unread,
        out_specs=jax.tree.map(lambda _: vmem, out_shape),
        scratch_shapes=[pltpu.VMEM(shape, F32) for shape in scratch] + list(more),
        compiler_params=pltpu.CompilerParams(vmem_limit_bytes=limit * 2**20),
        name=name,
    )(*args)


def near_kernel(x_ref, out_ref, sem):
    copy = pltpu.make_async_copy(x_ref, out_ref, sem)
    copy.start()
    copy.wait()


def near(x, name):
    return call(near_kernel, name, like(x.shape, x.dtype), [], x, unread=1, more=[pltpu.SemaphoreType.DMA])


def like(shape, dtype):
    return jax.ShapeDtypeStruct(shape, dtype)


def rows_kernel(x_ref, out_ref, rows_s):
    groups, rows, width = x_ref.shape
    for g in range(groups):
        rows_s[g * rows : (g + 1) * rows, :] = x_ref[g].astype(F32)
    x = rows_s[...]
    scale = lax.rsqrt(jnp.mean(x * x, axis=-1, keepdims=True) + 1e-05)
    first = scale.astype(BF16).astype(F32)
    second = (scale - first).astype(BF16).astype(F32)
    lane = lax.broadcasted_iota(jnp.int32, (groups * rows, 128), 1)
    more = jnp.zeros((groups * rows, 128), F32)
    for at, value in enumerate((first, second, scale - first - second)):
        more = jnp.where(lane == at, value, more)
    for h in range(out_ref.shape[0]):
        out_ref[h, :, 0:width] = x.astype(BF16)
        out_ref[h, :, width:] = more.astype(BF16)


def normed_rows(x_ref, gain_ref, width):
    normed = []
    for h in range(x_ref.shape[0]):
        more = x_ref[h, :, width:].astype(F32)
        scale = more[:, 0:1] + more[:, 1:2] + more[:, 2:3]
        normed.append((x_ref[h, :, 0:width].astype(F32) * scale * gain_ref[...]).astype(BF16))
    return jnp.concatenate(normed, 0)


def in_order(source, target, quarters):
    part = source.shape[0] // quarters
    groups = part // MOST
    for h in range(quarters):
        for r in range(MOST):
            own = source[pl.ds(h * part + r, groups, stride=MOST), :]
            target[pl.ds(h * MOST + r, groups, stride=quarters * MOST), :] = own


def project_kernel(x_ref, gain_ref, w_ref, stream_ref, tail_ref, mixed_s, stream_s):
    quarters, part, _ = x_ref.shape
    normed = normed_rows(x_ref, gain_ref, w_ref.shape[0])
    mixed_s[...] = jnp.dot(normed, w_ref[...], preferred_element_type=F32)
    in_order(mixed_s, stream_s, quarters)
    stream_ref[...] = stream_s[...].astype(BF16)
    tail_ref[...] = stream_s[quarters * part - 8 :, :].astype(BF16).astype(F32)


def project_gate_kernel(x_ref, gain_ref, w_ref, gate_ref, mixed_s, gate_s):
    normed = normed_rows(x_ref, gain_ref, w_ref.shape[0])
    mixed_s[...] = jnp.dot(normed, w_ref[...], preferred_element_type=F32)
    in_order(mixed_s, gate_s, x_ref.shape[0])
    gate_ref[...] = gate_s[...].astype(BF16)


def conv_kernel(stream_ref, halo_ref, params_ref, wx_ref, act_ref, tile_ref, pad_s, wide_s, tile_s):
    tokens, channels = stream_ref.shape
    pad_s[0:8, :] = halo_ref[...]
    pad_s[8:, :] = stream_ref[...].astype(F32)
    conv = params_ref[BIAS : BIAS + 1, :] + jnp.zeros((tokens, channels), F32)
    for k in range(CONV):
        at = 8 - (CONV - 1) + k
        conv = conv + params_ref[TAPS + k : TAPS + k + 1, :] * pad_s[at : at + tokens, :]
    act = silu(conv).astype(BF16)
    act_ref[...] = act
    wide = jnp.dot(act, wx_ref[...], preferred_element_type=F32)
    blocks = wide_s.shape[0]
    for i in range(blocks):
        wide_s[i] = wide[:, i * 128 : i * 128 + 128]
    groups = tile_ref.shape[0]
    maps = jnp.zeros((groups, 128), F32)
    for r in range(MOST):
        own = pl.ds(r, groups, stride=MOST)
        for c in range(2):
            tile_s[pl.ds(2 * r + c, groups, stride=8), :] = wide_s[c, own, :]
        maps = maps + wide_s[2 + r, own, :]
    tile_s[pl.ds(6, groups, stride=8), :] = maps
    tile_s[pl.ds(7, groups, stride=8), :] = jnp.zeros((groups, 128), F32)
    tile_ref[...] = tile_s[...].reshape(groups, 8, 128).astype(BF16)


def tile_sum_kernel(got_ref, route_ref, _0, out_ref):
    total = jnp.sum(got_ref[...].astype(F32), axis=0)
    row = lax.broadcasted_iota(jnp.int32, total.shape, 0)
    total = jnp.where(row == 7, route_ref[...], total).astype(BF16)
    out_ref[...] = jnp.broadcast_to(total[None], out_ref.shape)


def scan_kernel(back_ref, wdt_ref, params_ref, act_ref, out_ref, send_ref, tile_s, low_s, step_s, drive_s):
    _, tokens, half = low_s.shape
    groups = back_ref.shape[0]
    tile_s[...] = back_ref[...].astype(F32).reshape(groups * 8, 128)
    for r in range(MOST):
        for c in range(2):
            low_s[c, pl.ds(r, groups, stride=MOST), :] = tile_s[pl.ds(2 * r + c, groups, stride=8), :]
    blank = jnp.zeros((128 - groups, 128), F32)
    maps = jnp.concatenate([tile_s[pl.ds(6, groups, stride=8), :], blank], 0).T
    routes = jnp.concatenate([tile_s[pl.ds(7, groups, stride=8), :], blank], 0).T
    out_ref[2 * tokens :, :] = maps
    decay = -jnp.exp(params_ref[0:STATES, :])
    states, channels = decay.shape
    step = jnp.dot(low_s[0].astype(BF16), wdt_ref[0:half, :], preferred_element_type=F32)
    step = step + jnp.dot(low_s[1].astype(BF16), wdt_ref[half:, :], preferred_element_type=F32)
    step = softplus(step + params_ref[STEP : STEP + 1, :])
    step_s[...] = step
    act = act_ref[...].astype(F32)
    drive_s[...] = step * act
    state = jnp.zeros((states, channels), F32)
    total = jnp.zeros((1, channels), F32)
    for t in range(tokens):
        at, own = t % MOST * 32, t // MOST
        step_t = step_s[t : t + 1, :]
        b_t = jnp.broadcast_to(maps[at : at + 16, own : own + 1], (states, channels))
        c_t = jnp.broadcast_to(maps[at + 16 : at + 32, own : own + 1], (states, channels))
        state = jnp.exp(step_t * decay) * state + drive_s[t : t + 1, :] * b_t
        total = total + step_t
        out_ref[t : t + 1, :] = jnp.sum(c_t * state, axis=0, keepdims=True)
        out_ref[tokens + t : tokens + t + 1, :] = total
    out_ref[0:tokens, :] = out_ref[0:tokens, :] + params_ref[SKIP : SKIP + 1, :] * act
    routes = jnp.concatenate([routes[0:6, 0:groups], routes[6:12, 0:groups]], 1)
    tail = jnp.concatenate([total, routes, jnp.zeros((1, channels), F32)], 0)
    for k in range(send_ref.shape[0]):
        send_ref[k, 0:states, :] = state
        send_ref[k, states:, :] = tail


def gate_kernel(me_ref, all_ref, params_ref, local_ref, z_ref, out_ref, corr_s):
    tokens = z_ref.shape[0]
    decay = -jnp.exp(params_ref[0:STATES, :])
    states, channels = decay.shape
    state = jnp.zeros((states, channels), F32)
    me = me_ref[0]
    for k in range(all_ref.shape[0] - 1):
        total = all_ref[k, states : states + 1, :]
        later = jnp.exp(total * decay) * state + all_ref[k, 0:states, :]
        state = jnp.where(k < me, later, state)
    maps = local_ref[2 * tokens :, :]
    for t in range(tokens):
        at, own = t % MOST * 32 + 16, t // MOST
        c_t = jnp.broadcast_to(maps[at : at + 16, own : own + 1], (states, channels))
        term = c_t * (jnp.exp(local_ref[tokens + t : tokens + t + 1, :] * decay) * state)
        corr_s[t : t + 1, :] = jnp.sum(term, axis=0, keepdims=True)
    z = z_ref[...].astype(F32)
    ssm = local_ref[0:tokens, :] + corr_s[...]
    gated = (ssm * silu(z)).astype(BF16)
    for h in range(out_ref.shape[0]):
        out_ref[h] = gated


def mix_kernel(gated_ref, w_ref, _0, out_ref, mixed_s):
    quarters = gated_ref.shape[0]
    per = w_ref.shape[0] // quarters
    cols = w_ref.shape[2]
    for b in range(per):
        total = jnp.dot(gated_ref[0], w_ref[b], preferred_element_type=F32)
        for h in range(1, quarters):
            total = total + jnp.dot(gated_ref[h], w_ref[h * per + b], preferred_element_type=F32)
        mixed_s[:, b * cols : (b + 1) * cols] = total
    block = mixed_s.shape[0] // out_ref.shape[0]
    wide = mixed_s.shape[1]
    for j in range(out_ref.shape[0]):
        own = mixed_s[j * block : (j + 1) * block, :]
        rest = jnp.concatenate([own[8:, : wide // 2], own[8:, wide // 2 :]], 0)
        out_ref[j] = jnp.concatenate([own[:8], rest], 1).astype(BF16)


def resid_kernel(parts_ref, x_ref, select_ref, resid_ref, send_ref, wide_s):
    block, cols = resid_ref.shape
    sums = jnp.sum(parts_ref[...].astype(F32), axis=0)
    rest = jnp.concatenate([sums[: block - 8, cols:], sums[block - 8 :, cols:]], 1)
    total = x_ref[...].astype(F32) + jnp.concatenate([sums[:, :cols], rest], 0)
    resid = total.astype(BF16)
    resid_ref[...] = resid
    wide_s[...] = jnp.zeros_like(wide_s)
    wide_s[0:block, :] = resid.astype(F32)
    send = jnp.dot(select_ref[...], wide_s[...].astype(BF16), preferred_element_type=F32)
    for e in range(send_ref.shape[0]):
        own = send[e * MOST : (e + 1) * MOST]
        rows = [own[:, 0:384], own[:, 384:768]]
        rows.append(jnp.concatenate([own[0:1, 768:], own[2:3, 768:896]], 1))
        rows.append(jnp.concatenate([own[1:2, 768:], own[2:3, 896:]], 1))
        send_ref[e] = jnp.concatenate(rows, 0).astype(BF16)


def slots_kernel(got_ref, _0, out_ref, slots_s):
    for j in range(got_ref.shape[0]):
        own = got_ref[j].astype(F32)
        at = j * MOST
        slots_s[at : at + 3, 0:384] = own[0:3]
        slots_s[at : at + 3, 384:768] = own[3:6]
        slots_s[at : at + 1, 768:] = own[6:7, 0:256]
        slots_s[at + 1 : at + 2, 768:] = own[7:8, 0:256]
        slots_s[at + 2 : at + 3, 768:] = jnp.concatenate([own[6:7, 256:], own[7:8, 256:]], 1)
    out_ref[...] = slots_s[...].astype(BF16)


def stage_kernel(w0_ref, w1_ref, w2_ref, w3_ref, out_ref, sems):
    hidden = w1_ref.shape[1]
    copies = []
    for d, w_ref in enumerate((w0_ref, w1_ref, w2_ref, w3_ref)):
        copies.append(pltpu.make_async_copy(w_ref, out_ref.at[:, pl.ds(d * hidden, hidden)], sems.at[d]))
        copies[d].start()
    for copy in copies:
        copy.wait()


def expert_kernel(me_ref, tok_ref, gain_ref, resid_ref, w_ref, out_ref):
    me = me_ref[0]
    slots, cols = tok_ref.shape
    quarters = out_ref.shape[0]
    hidden = w_ref.shape[1] // quarters
    tok = tok_ref[...].astype(F32)
    sums = jnp.sum(tok * tok, axis=-1, keepdims=True)
    sums = jnp.broadcast_to(sums, (slots, 128)).T[0:MOST]
    first = sums.astype(BF16).astype(F32)
    second = (sums - first).astype(BF16).astype(F32)
    third = sums - first - second
    row = lax.broadcasted_iota(jnp.int32, (MOST, slots), 0)
    scales = jnp.where(row == 0, first, jnp.where(row == 1, second, third))
    resid = resid_ref[...].astype(F32)
    rows = resid.shape[0] // quarters
    for h in range(quarters):
        pieces = [scales]
        for r in range(rows):
            own = resid[h * rows + r : h * rows + r + 1, :]
            pieces.append(own[:, 0:hidden])
            pieces.append(own[:, hidden : 2 * hidden])
            pieces.append(jnp.concatenate([own[:, 2 * hidden :], jnp.zeros((1, 3 * hidden - cols), F32)], 1))
        pieces.append(jnp.zeros((16 - 4 * MOST, hidden), F32))
        out_ref[h, slots:, :] = jnp.concatenate(pieces, 0).astype(BF16)
    tok = (tok * gain_ref[...]).astype(BF16)
    for d in range(0, quarters, 2):
        pair = jnp.dot(tok, w_ref[:, d * hidden : (d + 2) * hidden], preferred_element_type=F32).astype(BF16)
        for i in range(2):
            out_ref[lax.rem(me - d - i + quarters, quarters), 0:slots, :] = pair[:, i * hidden : (i + 1) * hidden]


def finish_kernel(part_ref, wts_ref, out_ref, resid_ref, resid_s):
    quarters, _, hidden = part_ref.shape
    slots = out_ref.shape[0]
    rows, width = resid_ref.shape
    cols = width // quarters
    total = jnp.zeros((slots, hidden), F32)
    squares = jnp.zeros((1, slots), F32)
    for q in range(quarters):
        total = total + part_ref[q, 0:slots, :].astype(F32)
        own = part_ref[q, slots:, :].astype(F32)
        squares = squares + (own[0:1] + own[1:2] + own[2:3])
        for r in range(rows):
            for m in range(3):
                size = min(hidden, cols - m * hidden)
                at = q * cols + m * hidden
                resid_s[r : r + 1, at : at + size] = own[3 + 3 * r + m : 4 + 3 * r + m, 0:size]
    resid_ref[...] = resid_s[0:rows, :].astype(BF16)
    row = lax.broadcasted_iota(jnp.int32, (8, slots), 0)
    scale = lax.rsqrt(squares / width + 1e-05)
    both = jnp.where(row == 0, scale, wts_ref[...]).T
    out_ref[...] = (silu(total * both[:, 0:1]) * both[:, 1:2]).astype(BF16)


def shards(
    x_in,
    norm_gain,
    w_in_x,
    w_in_z,
    conv_weight,
    conv_bias,
    w_xproj,
    w_dt,
    dt_bias,
    a_log,
    d_skip,
    w_out,
    moe_gain,
    route_ids,
    route_weights,
    w_gate,
):
    n_seq, n_exp, n_hid = (lax.axis_size(a) for a in ("seq", "exp", "hid"))
    at_seq, at_exp, at_hid = (lax.axis_index(a) for a in ("seq", "exp", "hid"))
    rows, width = x_in.shape
    tokens = rows * n_exp * n_hid
    channels = w_in_x.shape[1]
    states = a_log.shape[0]
    rank = w_dt.shape[0]
    block = rows * n_hid
    cols = width // n_hid
    per = n_seq // n_hid

    w_x = lax.all_gather(w_in_x, "seq", axis=0, tiled=True)

    over_exp = lax.all_gather(x_in, "exp", axis=0, tiled=False)
    quarter_rows = call(
        rows_kernel,
        "rows",
        like((n_hid, n_exp * rows, width + 128), BF16),
        [(n_exp * rows, width)],
        over_exp,
    )
    quarter_rows, w_out, w_in_z = lax.optimization_barrier((quarter_rows, w_out, w_in_z))
    w_z = lax.all_gather(w_in_z, "seq", axis=0, tiled=True)
    route = [
        (s * n_hid + h, (h * per + s % per) * n_hid + s // per) for s in range(n_seq) for h in range(n_hid)
    ]
    w_out_here = lax.ppermute(w_out, ("seq", "hid"), route)
    w_maps = w_xproj[:, rank:]
    w_maps = jnp.concatenate(
        [w_xproj[:, :rank]] + [jnp.pad(w_maps, ((0, 0), (32 * r, 96 - 32 * r))) for r in range(rows)], 1
    )
    routes = jnp.concatenate([route_ids.astype(F32), route_weights.astype(F32)], 1).T.reshape(1, -1)
    routes = jnp.pad(routes, ((0, 0), (0, 128 - routes.shape[1])))
    params = jnp.concatenate(
        [a_log, conv_weight, conv_bias[None], dt_bias[None], d_skip[None], jnp.zeros((1, channels), F32)], 0
    )
    all_rows = exchange(quarter_rows, "hid")
    x_block = lax.dynamic_slice(
        all_rows.reshape(n_hid, n_exp, rows, -1), (0, at_exp, 0, at_hid * cols), (n_hid, 1, rows, cols)
    ).reshape(block, cols)
    stream, tail = call(
        project_kernel,
        "project",
        (like((tokens, channels), BF16), like((8, channels), F32)),
        [(tokens, channels), (tokens, channels)],
        all_rows,
        norm_gain[None],
        near(w_x, "near_x"),
    )
    gate_in = call(
        project_gate_kernel,
        "project_gate",
        like((tokens, channels), BF16),
        [(tokens, channels), (tokens, channels)],
        all_rows,
        norm_gain[None],
        w_z,
    )
    halo = lax.ppermute(tail, "seq", [(i, i + 1) for i in range(n_seq - 1)])
    inner_act, tiles = call(
        conv_kernel,
        "conv",
        (like((tokens, channels), BF16), like((n_exp * n_hid, 8, 128), BF16)),
        [(tokens + 8, channels), (5, tokens, 128), (n_exp * n_hid * 8, 128)],
        stream,
        halo,
        params,
        w_maps,
    )

    tiles, w_out_here = lax.optimization_barrier((tiles, w_out_here))
    w_out_all = lax.all_gather(w_out_here, "seq", axis=0, tiled=False)
    got = exchange(tiles, ("exp", "hid"))
    back = exchange(call(tile_sum_kernel, "tile_sum", like(got.shape, BF16), [], got, routes, gate_in, unread=1), ("exp", "hid"))

    def pick(w, d):
        return lax.dynamic_index_in_dim(w[0].reshape(n_hid, cols, -1), (at_hid + d) % n_hid, 0, keepdims=False)

    def shift(w, d):
        return lax.ppermute(pick(w, d), "hid", [(i, (i + d) % n_hid) for i in range(n_hid)])

    gate_in, w_first = lax.optimization_barrier((gate_in, w_gate))
    w_2 = shift(w_first, 2)
    local, carried = call(
        scan_kernel,
        "scan",
        (
            like((2 * tokens + 128, channels), F32),
            like((n_seq, states + 8, channels), F32),
        ),
        [(n_exp * n_hid * 8, 128), (2, tokens, 128), (tokens, channels), (tokens, channels)],
        back,
        w_dt,
        params,
        inner_act,
    )
    carried_all = exchange(carried, "seq")

    routed = carried_all[:, states + 1 : states + 7].reshape(n_seq, 6, 2, -1).transpose(0, 2, 1, 3)
    routed = routed.reshape(n_seq, 4, rows, -1).transpose(0, 3, 2, 1).reshape(n_seq * n_exp, block, 4)
    rows_ids = routed[:, :, :2].reshape(n_seq * n_exp, -1)
    rows_wts = routed[:, :, 2:].reshape(n_seq * n_exp, -1)
    n_rows = rows_ids.shape[1]
    upto = (jnp.arange(n_rows)[:, None] <= jnp.arange(n_rows)[None, :]).astype(F32)
    named = (rows_ids == at_exp.astype(F32)).astype(F32)
    place = jnp.dot(named, upto) * named
    weights = jnp.stack(
        [jnp.sum(jnp.where(place == i + 1.0, rows_wts, 0.0), 1) for i in range(MOST)], 1
    ).reshape(1, -1)
    ids = lax.dynamic_index_in_dim(rows_ids, at_seq * n_exp + at_exp, 0, keepdims=False)
    onehot = (ids[:, None] == jnp.arange(n_exp, dtype=F32)[None, :]).astype(F32)
    position = jnp.sum(jnp.dot(upto.T, onehot) * onehot, 1) - 1.0
    target = ids * MOST + position
    select = (target[None, :] == jnp.arange(n_exp * MOST, dtype=F32)[:, None]).astype(F32)
    select = jnp.sum(select.reshape(n_exp * MOST, block, -1), 2)
    select = jnp.pad(select, ((0, 0), (0, 16 - block))).astype(BF16)
    gated = call(
        gate_kernel,
        "gate",
        like((n_hid, tokens, channels), BF16),
        [(tokens, channels)],
        at_seq.astype(jnp.int32)[None],
        carried_all,
        params,
        local,
        gate_in,
        scalars=1,
    )

    gated_all = exchange(gated, "hid")
    mixed = call(
        mix_kernel,
        "mix",
        like((n_exp, 8, block * cols // 8), BF16),
        [(tokens, cols)],
        gated_all,
        near(w_out_all, "near_out"),
        w_2,
        unread=1,
    )
    mixed, w_second = lax.optimization_barrier((mixed, w_gate))
    w_own, w_1, w_3 = pick(w_second, 0), shift(w_second, 1), shift(w_second, 3)
    sums = exchange(mixed, "exp")
    resid_part, send = call(
        resid_kernel,
        "resid",
        (like((block, cols), BF16), like((n_exp, 8, MOST * cols // 8), BF16)),
        [(16, cols)],
        sums,
        x_block,
        select,
    )

    hidden = w_gate.shape[2]
    w_side = call(
        stage_kernel,
        "stage",
        like((cols, n_hid * hidden), BF16),
        [],
        w_own,
        w_1,
        w_2,
        w_3,
        unread=4,
        more=[pltpu.SemaphoreType.DMA((n_hid,))],
    )
    slots = call(
        slots_kernel,
        "slots",
        like((n_exp * MOST, cols), BF16),
        [(n_exp * MOST, cols)],
        exchange(send, "exp"),
        w_side,
        unread=1,
    )
    all_slots = lax.all_gather(slots, "seq", axis=0, tiled=True)
    n_all = all_slots.shape[0]
    away = call(
        expert_kernel,
        "expert",
        like((n_hid, n_all + 16, hidden), BF16),
        [],
        at_hid.astype(jnp.int32)[None],
        all_slots,
        lax.dynamic_slice_in_dim(moe_gain, at_hid * cols, cols, 0)[None],
        resid_part,
        w_side,
        scalars=1,
    )
    home = exchange(away, "hid")
    activated, resid = call(
        finish_kernel,
        "finish",
        (like((n_all, hidden), BF16), like((rows, width), BF16)),
        [(8, width)],
        home,
        weights,
    )
    return (resid, activated[None])


def solution(mesh):
    in_specs = (
        P(("seq", "exp", "hid"), None),
        P(),
        P("seq", ("exp", "hid")),
        P("seq", ("exp", "hid")),
        P(None, ("exp", "hid")),
        P(("exp", "hid")),
        P(("exp", "hid"), None),
        P(None, ("exp", "hid")),
        P(("exp", "hid")),
        P(None, ("exp", "hid")),
        P(("exp", "hid")),
        P(("exp", "hid"), "seq"),
        P(),
        P(("seq", "exp", "hid"), None),
        P(("seq", "exp", "hid"), None),
        P("exp", None, ("seq", "hid")),
    )
    out_specs = (P(("seq", "exp", "hid"), None), P("exp", None, ("seq", "hid")))
    return jax.shard_map(shards, mesh=mesh, in_specs=in_specs, out_specs=out_specs, check_vma=False)
```

```python
import jax
import jax.numpy as jnp
from jax import lax
from jax.experimental import pallas as pl
from jax.experimental.pallas import tpu as pltpu
from jax.sharding import PartitionSpec as P

F32 = jnp.float32
BF16 = jnp.bfloat16
MOST = 3
STATES = 16
CONV = 4
TAPS, BIAS, STEP, SKIP = 16, 20, 21, 22


def exchange(x, axis):
    return lax.all_to_all(x, axis, split_axis=0, concat_axis=0, tiled=True)


def softplus(v):
    return jnp.maximum(v, 0.0) + jnp.log1p(jnp.exp(-jnp.abs(v)))


def silu(v):
    return v / (1.0 + jnp.exp(-v))


def call(body, name, out_shape, scratch, *args, scalars=0, unread=0, more=(), limit=40):
    vmem, smem = pl.BlockSpec(memory_space=pltpu.VMEM), pl.BlockSpec(memory_space=pltpu.SMEM)
    return pl.pallas_call(
        body,
        out_shape=out_shape,
        in_specs=[smem] * scalars
        + [vmem] * (len(args) - scalars - unread)
        + [pl.BlockSpec(memory_space=pl.ANY)] * unread,
        out_specs=jax.tree.map(lambda _: vmem, out_shape),
        scratch_shapes=[pltpu.VMEM(shape, F32) for shape in scratch] + list(more),
        compiler_params=pltpu.CompilerParams(vmem_limit_bytes=limit * 2**20),
        name=name,
    )(*args)


def near_kernel(x_ref, out_ref, sem):
    copy = pltpu.make_async_copy(x_ref, out_ref, sem)
    copy.start()
    copy.wait()


def near(x, name):
    return call(near_kernel, name, like(x.shape, x.dtype), [], x, unread=1, more=[pltpu.SemaphoreType.DMA])


def like(shape, dtype):
    return jax.ShapeDtypeStruct(shape, dtype)


def rows_kernel(x_ref, out_ref, rows_s):
    groups, rows, width = x_ref.shape
    for g in range(groups):
        rows_s[g * rows : (g + 1) * rows, :] = x_ref[g].astype(F32)
    x = rows_s[...]
    scale = lax.rsqrt(jnp.mean(x * x, axis=-1, keepdims=True) + 1e-05)
    first = scale.astype(BF16).astype(F32)
    second = (scale - first).astype(BF16).astype(F32)
    lane = lax.broadcasted_iota(jnp.int32, (groups * rows, 128), 1)
    more = jnp.zeros((groups * rows, 128), F32)
    for at, value in enumerate((first, second, scale - first - second)):
        more = jnp.where(lane == at, value, more)
    for h in range(out_ref.shape[0]):
        out_ref[h, :, 0:width] = x.astype(BF16)
        out_ref[h, :, width:] = more.astype(BF16)


def normed_rows(x_ref, gain_ref, width):
    normed = []
    for h in range(x_ref.shape[0]):
        more = x_ref[h, :, width:].astype(F32)
        scale = more[:, 0:1] + more[:, 1:2] + more[:, 2:3]
        normed.append((x_ref[h, :, 0:width].astype(F32) * scale * gain_ref[...]).astype(BF16))
    return jnp.concatenate(normed, 0)


def in_order(source, target, quarters):
    part = source.shape[0] // quarters
    groups = part // MOST
    for h in range(quarters):
        for r in range(MOST):
            own = source[pl.ds(h * part + r, groups, stride=MOST), :]
            target[pl.ds(h * MOST + r, groups, stride=quarters * MOST), :] = own


def project_kernel(x_ref, gain_ref, w_ref, stream_ref, tail_ref, mixed_s, stream_s):
    quarters, part, _ = x_ref.shape
    normed = normed_rows(x_ref, gain_ref, w_ref.shape[0])
    mixed_s[...] = jnp.dot(normed, w_ref[...], preferred_element_type=F32)
    in_order(mixed_s, stream_s, quarters)
    stream_ref[...] = stream_s[...].astype(BF16)
    tail_ref[...] = stream_s[quarters * part - 8 :, :].astype(BF16).astype(F32)


def project_gate_kernel(x_ref, gain_ref, w_ref, gate_ref, mixed_s, gate_s):
    normed = normed_rows(x_ref, gain_ref, w_ref.shape[0])
    mixed_s[...] = jnp.dot(normed, w_ref[...], preferred_element_type=F32)
    in_order(mixed_s, gate_s, x_ref.shape[0])
    gate_ref[...] = gate_s[...].astype(BF16)


def conv_kernel(stream_ref, halo_ref, params_ref, wx_ref, act_ref, tile_ref, pad_s, wide_s, tile_s):
    tokens, channels = stream_ref.shape
    pad_s[0:8, :] = halo_ref[...]
    pad_s[8:, :] = stream_ref[...].astype(F32)
    conv = params_ref[BIAS : BIAS + 1, :] + jnp.zeros((tokens, channels), F32)
    for k in range(CONV):
        at = 8 - (CONV - 1) + k
        conv = conv + params_ref[TAPS + k : TAPS + k + 1, :] * pad_s[at : at + tokens, :]
    act = silu(conv).astype(BF16)
    act_ref[...] = act
    wide = jnp.dot(act, wx_ref[...], preferred_element_type=F32)
    blocks = wide_s.shape[0]
    for i in range(blocks):
        wide_s[i] = wide[:, i * 128 : i * 128 + 128]
    groups = tile_ref.shape[0]
    maps = jnp.zeros((groups, 128), F32)
    for r in range(MOST):
        own = pl.ds(r, groups, stride=MOST)
        for c in range(2):
            tile_s[pl.ds(2 * r + c, groups, stride=8), :] = wide_s[c, own, :]
        maps = maps + wide_s[2 + r, own, :]
    tile_s[pl.ds(6, groups, stride=8), :] = maps
    tile_s[pl.ds(7, groups, stride=8), :] = jnp.zeros((groups, 128), F32)
    tile_ref[...] = tile_s[...].reshape(groups, 8, 128).astype(BF16)


def tile_sum_kernel(got_ref, route_ref, _0, out_ref):
    total = jnp.sum(got_ref[...].astype(F32), axis=0)
    row = lax.broadcasted_iota(jnp.int32, total.shape, 0)
    total = jnp.where(row == 7, route_ref[...], total).astype(BF16)
    out_ref[...] = jnp.broadcast_to(total[None], out_ref.shape)


def scan_kernel(back_ref, wdt_ref, params_ref, act_ref, out_ref, send_ref, tile_s, low_s, step_s, drive_s):
    _, tokens, half = low_s.shape
    groups = back_ref.shape[0]
    tile_s[...] = back_ref[...].astype(F32).reshape(groups * 8, 128)
    for r in range(MOST):
        for c in range(2):
            low_s[c, pl.ds(r, groups, stride=MOST), :] = tile_s[pl.ds(2 * r + c, groups, stride=8), :]
    blank = jnp.zeros((128 - groups, 128), F32)
    maps = jnp.concatenate([tile_s[pl.ds(6, groups, stride=8), :], blank], 0).T
    routes = jnp.concatenate([tile_s[pl.ds(7, groups, stride=8), :], blank], 0).T
    out_ref[2 * tokens :, :] = maps
    decay = -jnp.exp(params_ref[0:STATES, :])
    states, channels = decay.shape
    step = jnp.dot(low_s[0].astype(BF16), wdt_ref[0:half, :], preferred_element_type=F32)
    step = step + jnp.dot(low_s[1].astype(BF16), wdt_ref[half:, :], preferred_element_type=F32)
    step = softplus(step + params_ref[STEP : STEP + 1, :])
    step_s[...] = step
    act = act_ref[...].astype(F32)
    drive_s[...] = step * act
    state = jnp.zeros((states, channels), F32)
    total = jnp.zeros((1, channels), F32)
    for t in range(tokens):
        at, own = t % MOST * 32, t // MOST
        step_t = step_s[t : t + 1, :]
        b_t = jnp.broadcast_to(maps[at : at + 16, own : own + 1], (states, channels))
        c_t = jnp.broadcast_to(maps[at + 16 : at + 32, own : own + 1], (states, channels))
        state = jnp.exp(step_t * decay) * state + drive_s[t : t + 1, :] * b_t
        total = total + step_t
        out_ref[t : t + 1, :] = jnp.sum(c_t * state, axis=0, keepdims=True)
        out_ref[tokens + t : tokens + t + 1, :] = total
    out_ref[0:tokens, :] = out_ref[0:tokens, :] + params_ref[SKIP : SKIP + 1, :] * act
    routes = jnp.concatenate([routes[0:6, 0:groups], routes[6:12, 0:groups]], 1)
    tail = jnp.concatenate([total, routes, jnp.zeros((1, channels), F32)], 0)
    for k in range(send_ref.shape[0]):
        send_ref[k, 0:states, :] = state
        send_ref[k, states:, :] = tail


def gate_kernel(me_ref, all_ref, params_ref, local_ref, z_ref, out_ref, corr_s):
    tokens = z_ref.shape[0]
    decay = -jnp.exp(params_ref[0:STATES, :])
    states, channels = decay.shape
    state = jnp.zeros((states, channels), F32)
    me = me_ref[0]
    for k in range(all_ref.shape[0] - 1):
        total = all_ref[k, states : states + 1, :]
        later = jnp.exp(total * decay) * state + all_ref[k, 0:states, :]
        state = jnp.where(k < me, later, state)
    maps = local_ref[2 * tokens :, :]
    for t in range(tokens):
        at, own = t % MOST * 32 + 16, t // MOST
        c_t = jnp.broadcast_to(maps[at : at + 16, own : own + 1], (states, channels))
        term = c_t * (jnp.exp(local_ref[tokens + t : tokens + t + 1, :] * decay) * state)
        corr_s[t : t + 1, :] = jnp.sum(term, axis=0, keepdims=True)
    z = z_ref[...].astype(F32)
    ssm = local_ref[0:tokens, :] + corr_s[...]
    gated = (ssm * silu(z)).astype(BF16)
    for h in range(out_ref.shape[0]):
        out_ref[h] = gated


def mix_kernel(gated_ref, w_ref, _0, out_ref, mixed_s):
    quarters = gated_ref.shape[0]
    per = w_ref.shape[0] // quarters
    cols = w_ref.shape[2]
    for b in range(per):
        total = jnp.dot(gated_ref[0], w_ref[b], preferred_element_type=F32)
        for h in range(1, quarters):
            total = total + jnp.dot(gated_ref[h], w_ref[h * per + b], preferred_element_type=F32)
        mixed_s[:, b * cols : (b + 1) * cols] = total
    block = mixed_s.shape[0] // out_ref.shape[0]
    wide = mixed_s.shape[1]
    for j in range(out_ref.shape[0]):
        own = mixed_s[j * block : (j + 1) * block, :]
        rest = jnp.concatenate([own[8:, : wide // 2], own[8:, wide // 2 :]], 0)
        out_ref[j] = jnp.concatenate([own[:8], rest], 1).astype(BF16)


def resid_kernel(parts_ref, x_ref, select_ref, resid_ref, send_ref, wide_s):
    block, cols = resid_ref.shape
    sums = jnp.sum(parts_ref[...].astype(F32), axis=0)
    rest = jnp.concatenate([sums[: block - 8, cols:], sums[block - 8 :, cols:]], 1)
    total = x_ref[...].astype(F32) + jnp.concatenate([sums[:, :cols], rest], 0)
    resid = total.astype(BF16)
    resid_ref[...] = resid
    wide_s[...] = jnp.zeros_like(wide_s)
    wide_s[0:block, :] = resid.astype(F32)
    send = jnp.dot(select_ref[...], wide_s[...].astype(BF16), preferred_element_type=F32)
    for e in range(send_ref.shape[0]):
        own = send[e * MOST : (e + 1) * MOST]
        rows = [own[:, 0:384], own[:, 384:768]]
        rows.append(jnp.concatenate([own[0:1, 768:], own[2:3, 768:896]], 1))
        rows.append(jnp.concatenate([own[1:2, 768:], own[2:3, 896:]], 1))
        send_ref[e] = jnp.concatenate(rows, 0).astype(BF16)


def slots_kernel(got_ref, _0, out_ref, slots_s):
    for j in range(got_ref.shape[0]):
        own = got_ref[j].astype(F32)
        at = j * MOST
        slots_s[at : at + 3, 0:384] = own[0:3]
        slots_s[at : at + 3, 384:768] = own[3:6]
        slots_s[at : at + 1, 768:] = own[6:7, 0:256]
        slots_s[at + 1 : at + 2, 768:] = own[7:8, 0:256]
        slots_s[at + 2 : at + 3, 768:] = jnp.concatenate([own[6:7, 256:], own[7:8, 256:]], 1)
    out_ref[...] = slots_s[...].astype(BF16)


def stage_kernel(w0_ref, w1_ref, w2_ref, w3_ref, out_ref, sems):
    hidden = w1_ref.shape[1]
    copies = []
    for d, w_ref in enumerate((w0_ref, w1_ref, w2_ref, w3_ref)):
        copies.append(pltpu.make_async_copy(w_ref, out_ref.at[:, pl.ds(d * hidden, hidden)], sems.at[d]))
        copies[d].start()
    for copy in copies:
        copy.wait()


def expert_kernel(me_ref, tok_ref, gain_ref, resid_ref, w_ref, out_ref):
    me = me_ref[0]
    slots, cols = tok_ref.shape
    quarters = out_ref.shape[0]
    hidden = w_ref.shape[1] // quarters
    tok = tok_ref[...].astype(F32)
    sums = jnp.sum(tok * tok, axis=-1, keepdims=True)
    sums = jnp.broadcast_to(sums, (slots, 128)).T[0:MOST]
    first = sums.astype(BF16).astype(F32)
    second = (sums - first).astype(BF16).astype(F32)
    third = sums - first - second
    row = lax.broadcasted_iota(jnp.int32, (MOST, slots), 0)
    scales = jnp.where(row == 0, first, jnp.where(row == 1, second, third))
    resid = resid_ref[...].astype(F32)
    rows = resid.shape[0] // quarters
    for h in range(quarters):
        pieces = [scales]
        for r in range(rows):
            own = resid[h * rows + r : h * rows + r + 1, :]
            pieces.append(own[:, 0:hidden])
            pieces.append(own[:, hidden : 2 * hidden])
            pieces.append(jnp.concatenate([own[:, 2 * hidden :], jnp.zeros((1, 3 * hidden - cols), F32)], 1))
        pieces.append(jnp.zeros((16 - 4 * MOST, hidden), F32))
        out_ref[h, slots:, :] = jnp.concatenate(pieces, 0).astype(BF16)
    tok = (tok * gain_ref[...]).astype(BF16)
    for d in range(0, quarters, 2):
        pair = jnp.dot(tok, w_ref[:, d * hidden : (d + 2) * hidden], preferred_element_type=F32).astype(BF16)
        for i in range(2):
            out_ref[lax.rem(me - d - i + quarters, quarters), 0:slots, :] = pair[:, i * hidden : (i + 1) * hidden]


def finish_kernel(part_ref, wts_ref, out_ref, resid_ref, resid_s):
    quarters, _, hidden = part_ref.shape
    slots = out_ref.shape[0]
    rows, width = resid_ref.shape
    cols = width // quarters
    total = jnp.zeros((slots, hidden), F32)
    squares = jnp.zeros((1, slots), F32)
    for q in range(quarters):
        total = total + part_ref[q, 0:slots, :].astype(F32)
        own = part_ref[q, slots:, :].astype(F32)
        squares = squares + (own[0:1] + own[1:2] + own[2:3])
        for r in range(rows):
            for m in range(3):
                size = min(hidden, cols - m * hidden)
                at = q * cols + m * hidden
                resid_s[r : r + 1, at : at + size] = own[3 + 3 * r + m : 4 + 3 * r + m, 0:size]
    resid_ref[...] = resid_s[0:rows, :].astype(BF16)
    row = lax.broadcasted_iota(jnp.int32, (8, slots), 0)
    scale = lax.rsqrt(squares / width + 1e-05)
    both = jnp.where(row == 0, scale, wts_ref[...]).T
    out_ref[...] = (silu(total * both[:, 0:1]) * both[:, 1:2]).astype(BF16)


def shards(
    x_in,
    norm_gain,
    w_in_x,
    w_in_z,
    conv_weight,
    conv_bias,
    w_xproj,
    w_dt,
    dt_bias,
    a_log,
    d_skip,
    w_out,
    moe_gain,
    route_ids,
    route_weights,
    w_gate,
):
    n_seq, n_exp, n_hid = (lax.axis_size(a) for a in ("seq", "exp", "hid"))
    at_seq, at_exp, at_hid = (lax.axis_index(a) for a in ("seq", "exp", "hid"))
    rows, width = x_in.shape
    tokens = rows * n_exp * n_hid
    channels = w_in_x.shape[1]
    states = a_log.shape[0]
    rank = w_dt.shape[0]
    block = rows * n_hid
    cols = width // n_hid
    per = n_seq // n_hid

    w_x = lax.all_gather(w_in_x, "seq", axis=0, tiled=True)

    over_exp = lax.all_gather(x_in, "exp", axis=0, tiled=False)
    quarter_rows = call(
        rows_kernel,
        "rows",
        like((n_hid, n_exp * rows, width + 128), BF16),
        [(n_exp * rows, width)],
        over_exp,
    )
    quarter_rows, w_out, w_in_z = lax.optimization_barrier((quarter_rows, w_out, w_in_z))
    w_z = lax.all_gather(w_in_z, "seq", axis=0, tiled=True)
    route = [
        (s * n_hid + h, (h * per + s % per) * n_hid + s // per) for s in range(n_seq) for h in range(n_hid)
    ]
    w_out_here = lax.ppermute(w_out, ("seq", "hid"), route)
    w_maps = w_xproj[:, rank:]
    w_maps = jnp.concatenate(
        [w_xproj[:, :rank]] + [jnp.pad(w_maps, ((0, 0), (32 * r, 96 - 32 * r))) for r in range(rows)], 1
    )
    routes = jnp.concatenate([route_ids.astype(F32), route_weights.astype(F32)], 1).T.reshape(1, -1)
    routes = jnp.pad(routes, ((0, 0), (0, 128 - routes.shape[1])))
    params = jnp.concatenate(
        [a_log, conv_weight, conv_bias[None], dt_bias[None], d_skip[None], jnp.zeros((1, channels), F32)], 0
    )
    all_rows = exchange(quarter_rows, "hid")
    x_block = lax.dynamic_slice(
        all_rows.reshape(n_hid, n_exp, rows, -1), (0, at_exp, 0, at_hid * cols), (n_hid, 1, rows, cols)
    ).reshape(block, cols)
    stream, tail = call(
        project_kernel,
        "project",
        (like((tokens, channels), BF16), like((8, channels), F32)),
        [(tokens, channels), (tokens, channels)],
        all_rows,
        norm_gain[None],
        near(w_x, "near_x"),
    )
    gate_in = call(
        project_gate_kernel,
        "project_gate",
        like((tokens, channels), BF16),
        [(tokens, channels), (tokens, channels)],
        all_rows,
        norm_gain[None],
        w_z,
    )
    halo = lax.ppermute(tail, "seq", [(i, i + 1) for i in range(n_seq - 1)])
    inner_act, tiles = call(
        conv_kernel,
        "conv",
        (like((tokens, channels), BF16), like((n_exp * n_hid, 8, 128), BF16)),
        [(tokens + 8, channels), (5, tokens, 128), (n_exp * n_hid * 8, 128)],
        stream,
        halo,
        params,
        w_maps,
    )

    got = exchange(tiles, ("exp", "hid"))
    got, w_out_here = lax.optimization_barrier((got, w_out_here))
    w_out_all = lax.all_gather(w_out_here, "seq", axis=0, tiled=False)
    back = exchange(call(tile_sum_kernel, "tile_sum", like(got.shape, BF16), [], got, routes, gate_in, unread=1), ("exp", "hid"))

    def pick(w, d):
        return lax.dynamic_index_in_dim(w[0].reshape(n_hid, cols, -1), (at_hid + d) % n_hid, 0, keepdims=False)

    def shift(w, d):
        return lax.ppermute(pick(w, d), "hid", [(i, (i + d) % n_hid) for i in range(n_hid)])

    gate_in, w_first = lax.optimization_barrier((gate_in, w_gate))
    w_2 = shift(w_first, 2)
    local, carried = call(
        scan_kernel,
        "scan",
        (
            like((2 * tokens + 128, channels), F32),
            like((n_seq, states + 8, channels), F32),
        ),
        [(n_exp * n_hid * 8, 128), (2, tokens, 128), (tokens, channels), (tokens, channels)],
        back,
        w_dt,
        params,
        inner_act,
    )
    carried_all = exchange(carried, "seq")

    routed = carried_all[:, states + 1 : states + 7].reshape(n_seq, 6, 2, -1).transpose(0, 2, 1, 3)
    routed = routed.reshape(n_seq, 4, rows, -1).transpose(0, 3, 2, 1).reshape(n_seq * n_exp, block, 4)
    rows_ids = routed[:, :, :2].reshape(n_seq * n_exp, -1)
    rows_wts = routed[:, :, 2:].reshape(n_seq * n_exp, -1)
    n_rows = rows_ids.shape[1]
    upto = (jnp.arange(n_rows)[:, None] <= jnp.arange(n_rows)[None, :]).astype(F32)
    named = (rows_ids == at_exp.astype(F32)).astype(F32)
    place = jnp.dot(named, upto) * named
    weights = jnp.stack(
        [jnp.sum(jnp.where(place == i + 1.0, rows_wts, 0.0), 1) for i in range(MOST)], 1
    ).reshape(1, -1)
    ids = lax.dynamic_index_in_dim(rows_ids, at_seq * n_exp + at_exp, 0, keepdims=False)
    onehot = (ids[:, None] == jnp.arange(n_exp, dtype=F32)[None, :]).astype(F32)
    position = jnp.sum(jnp.dot(upto.T, onehot) * onehot, 1) - 1.0
    target = ids * MOST + position
    select = (target[None, :] == jnp.arange(n_exp * MOST, dtype=F32)[:, None]).astype(F32)
    select = jnp.sum(select.reshape(n_exp * MOST, block, -1), 2)
    select = jnp.pad(select, ((0, 0), (0, 16 - block))).astype(BF16)
    gated = call(
        gate_kernel,
        "gate",
        like((n_hid, tokens, channels), BF16),
        [(tokens, channels)],
        at_seq.astype(jnp.int32)[None],
        carried_all,
        params,
        local,
        gate_in,
        scalars=1,
    )

    gated_all = exchange(gated, "hid")
    mixed = call(
        mix_kernel,
        "mix",
        like((n_exp, 8, block * cols // 8), BF16),
        [(tokens, cols)],
        gated_all,
        near(w_out_all, "near_out"),
        w_2,
        unread=1,
    )
    mixed, w_second = lax.optimization_barrier((mixed, w_gate))
    w_own, w_1, w_3 = pick(w_second, 0), shift(w_second, 1), shift(w_second, 3)
    sums = exchange(mixed, "exp")
    resid_part, send = call(
        resid_kernel,
        "resid",
        (like((block, cols), BF16), like((n_exp, 8, MOST * cols // 8), BF16)),
        [(16, cols)],
        sums,
        x_block,
        select,
    )

    hidden = w_gate.shape[2]
    w_side = call(
        stage_kernel,
        "stage",
        like((cols, n_hid * hidden), BF16),
        [],
        w_own,
        w_1,
        w_2,
        w_3,
        unread=4,
        more=[pltpu.SemaphoreType.DMA((n_hid,))],
    )
    slots = call(
        slots_kernel,
        "slots",
        like((n_exp * MOST, cols), BF16),
        [(n_exp * MOST, cols)],
        exchange(send, "exp"),
        w_side,
        unread=1,
    )
    all_slots = lax.all_gather(slots, "seq", axis=0, tiled=True)
    n_all = all_slots.shape[0]
    away = call(
        expert_kernel,
        "expert",
        like((n_hid, n_all + 16, hidden), BF16),
        [],
        at_hid.astype(jnp.int32)[None],
        all_slots,
        lax.dynamic_slice_in_dim(moe_gain, at_hid * cols, cols, 0)[None],
        resid_part,
        w_side,
        scalars=1,
    )
    home = exchange(away, "hid")
    activated, resid = call(
        finish_kernel,
        "finish",
        (like((n_all, hidden), BF16), like((rows, width), BF16)),
        [(8, width)],
        home,
        weights,
    )
    return (resid, activated[None])


def solution(mesh):
    in_specs = (
        P(("seq", "exp", "hid"), None),
        P(),
        P("seq", ("exp", "hid")),
        P("seq", ("exp", "hid")),
        P(None, ("exp", "hid")),
        P(("exp", "hid")),
        P(("exp", "hid"), None),
        P(None, ("exp", "hid")),
        P(("exp", "hid")),
        P(None, ("exp", "hid")),
        P(("exp", "hid")),
        P(("exp", "hid"), "seq"),
        P(),
        P(("seq", "exp", "hid"), None),
        P(("seq", "exp", "hid"), None),
        P("exp", None, ("seq", "hid")),
    )
    out_specs = (P(("seq", "exp", "hid"), None), P("exp", None, ("seq", "hid")))
    return jax.shard_map(shards, mesh=mesh, in_specs=in_specs, out_specs=out_specs, check_vma=False)
```
